32 devices in a mesh: parts: 2 (over y), pool: 4 (over z), tp: 2 (over x), sp: 2 (over core).
Axes of the slice: x: 2, y: 2, z: 4, core: 2. Of those that a mesh axis runs over, the one named last changes fastest.
Arguments:
- queries: bfloat16 [8, 256, 36864], P(('parts', 'pool'), 'sp', 'tp'), parts along dimension 0, may hold values from -32 to 32
- block_latent: bfloat16 [8, 256, 576], P(('parts', 'pool'), ('tp', 'sp')), parts along dimension 0, may hold values from -6 to 6
- prefix_cache: bfloat16 [8, 128, 576], P('parts', 'pool'), parts along dimension 0, may hold values from -6 to 6
- queue_list: int32 [8], P('parts'), parts along dimension 0, may hold values from 0 to 3, each once
- prefix_len: int32 [8], P('parts'), parts along dimension 0, may hold values from 32 to 128, as said below
- block_len: int32 [8], P('parts'), parts along dimension 0, may hold values from 64 to 256, as said below
- decode_dest: int32 [8], P('parts'), parts along dimension 0, may hold values from 0 to 3, as said below
Outputs:
- latent_out: bfloat16 [8, 256, 32768], P(('parts', 'pool'), 'sp', 'tp'), parts along dimension 0
- decode_pages: bfloat16 [8, 2, 6, 64, 576], P(('parts', 'pool'), None, None, ('tp', 'sp')), parts along dimension 0
The draws below stay inside these ranges and needn't reach their ends.
There are 2 independent parts, one for each index of `parts`. The reference program is written for one: setup_inputs(seed, part) draws one part's arguments, and reference() takes and returns one part's arrays. A program takes and returns all parts, laid end to end along the dimension named above; each array names one. Nothing has to cross between parts.
Inputs may be any that keep to these rules, and one draw needn't show every extreme that they name: `queue_list`: each request appears once. `prefix_len`: some request has exactly 128. `block_len`: some group has exactly 256. `decode_dest`: no decode group is named by more than 2 prefill groups, and some is named by exactly 2.
All inputs are finite; a program needn't handle non-finite values.
Results may differ from the reference program's by a relative error of at most 0.0034.
Values may be sent and summed in bfloat16 or wider, within the bound.
No kernel may reach another device: no remote copies, remote signals or barrier semaphores. Data moves between devices by JAX's collectives and lax.ppermute only.
A program may use at most 128 MiB of HBM per device.

```python
import jax
import jax.numpy as jnp
from jax import lax

LAT = 512
ROPE = 64
HEADS = 64
QK = 192
PG = 64
MOST = 2
GROUPS = 4
BLOCK = 256
PREFIX = 128
KEY_W = 576
CACHE = 384
PAGES = 6


def draw_block_latent(key, part):
    key = jax.random.fold_in(key, 5)
    latent = jnp.clip(jax.random.normal(key, (GROUPS, BLOCK, LAT + ROPE), jnp.float32), -6.0, 6.0)
    return latent.astype(jnp.bfloat16)


def draw_queries(key, part):
    key = jax.random.fold_in(key, 7)
    shape = (GROUPS, BLOCK, HEADS, LAT + ROPE)
    values = jnp.clip(jax.random.normal(key, shape, jnp.float32), -6.0, 6.0)
    return values.reshape(GROUPS, BLOCK, HEADS * (LAT + ROPE)).astype(jnp.bfloat16)


def draw_prefix_len(key, part):
    key = jax.random.fold_in(key, 11)
    key_values, key_spot = jax.random.split(key)
    values = jax.random.randint(key_values, (GROUPS,), PREFIX // 4, PREFIX + 1)
    forced_spot = jax.random.randint(key_spot, (), 0, GROUPS)
    return jnp.where(jnp.arange(GROUPS) == forced_spot, PREFIX, values).astype(jnp.int32)


def draw_block_len(key, part):
    key = jax.random.fold_in(key, 13)
    key_values, key_spot = jax.random.split(key)
    values = jax.random.randint(key_values, (GROUPS,), max(12, BLOCK // 4), BLOCK + 1)
    forced_spot = jax.random.randint(key_spot, (), 0, GROUPS)
    return jnp.where(jnp.arange(GROUPS) == forced_spot, BLOCK, values).astype(jnp.int32)


def draw_decode_dest(key, part):
    key = jax.random.fold_in(key, 17)
    key_order, key_full, key_assign = jax.random.split(key, 3)
    slot_total = GROUPS * MOST
    slot_ids = jnp.arange(slot_total, dtype=jnp.int32)
    order = jax.random.permutation(key_order, slot_total)
    position = jnp.zeros((slot_total,), jnp.int32).at[order].set(slot_ids)
    full_group = jax.random.randint(key_full, (), 0, GROUPS)
    score = jnp.where(slot_ids // MOST == full_group, slot_ids - slot_total, position)
    picked = jnp.argsort(score, stable=True)[:GROUPS]
    mixing = jax.random.permutation(key_assign, GROUPS)
    return (picked // MOST)[mixing].astype(jnp.int32)


def shard_levels(stream_key, extent, cuts, least, high):
    level, own = 1.0, jax.random.fold_in(stream_key, 6)
    for dim, shards_of in cuts:
        heights = jnp.exp(jax.random.uniform(jax.random.fold_in(own, dim), (shards_of,), jnp.float32, least / len(cuts), high / len(cuts)))
        level = level * jnp.repeat(heights, extent[dim] // shards_of).reshape([-1 if axis == dim else 1 for axis in range(len(extent))])
    return level


def noise(stream_key, extent, spread, reach, pieces=(), held_as=jnp.bfloat16):
    gain = shard_levels(stream_key, extent, pieces, -0.22, 0.18) if pieces else 1.0
    entries = jax.random.normal(stream_key, extent, jnp.float32) * spread * gain
    return jnp.minimum(jnp.maximum(entries, -reach), reach).astype(held_as)


def setup_inputs(seed: int = 0, part: int = 0) -> dict:
    streams_of = jax.random.split(jax.random.key(seed), 8)
    own_keys = jax.random.split(jax.random.fold_in(streams_of[7], part), 8)
    return {
        "queries": draw_queries(jax.random.fold_in(jax.random.fold_in(streams_of[7], part), 71), part),
        "block_latent": draw_block_latent(jax.random.fold_in(jax.random.fold_in(streams_of[7], part), 71), part),
        "prefix_cache": noise(own_keys[2], (GROUPS, PREFIX, KEY_W), 1.0, 6.0, ((1, 4),)),
        "queue_list": jax.random.permutation(own_keys[3], GROUPS).astype(jnp.int32),
        "prefix_len": draw_prefix_len(jax.random.fold_in(jax.random.fold_in(streams_of[7], part), 71), part),
        "block_len": draw_block_len(jax.random.fold_in(jax.random.fold_in(streams_of[7], part), 71), part),
        "decode_dest": draw_decode_dest(jax.random.fold_in(jax.random.fold_in(streams_of[7], part), 71), part),
    }


def group_attention(queries, all_keys, pre_length, blk_length):
    query_count = queries.shape[0]
    key_width = all_keys.shape[1]
    heads_all = queries.shape[1] // key_width
    query_rows = queries.reshape(query_count * heads_all, key_width)
    scores = jnp.dot(query_rows, all_keys.T, preferred_element_type=jnp.float32) * (QK ** -0.5)
    scores = scores.reshape(query_count, heads_all, all_keys.shape[0])
    key_index = jnp.arange(all_keys.shape[0], dtype=jnp.int32)
    query_index = jnp.arange(query_count, dtype=jnp.int32)
    new_index = key_index - PREFIX
    visible = jnp.where(key_index[None, :] < PREFIX, (key_index < pre_length)[None, :],
                        (new_index[None, :] <= query_index[:, None]) & (new_index < blk_length)[None, :])
    visible = visible[:, None, :]
    row_top = jnp.max(jnp.where(visible, scores, -jnp.inf), axis=2, keepdims=True)
    weights = jnp.where(visible, jnp.exp(scores - row_top), 0.0)
    row_total = jnp.sum(weights, axis=2, keepdims=True)
    rounded = weights.astype(jnp.bfloat16).reshape(query_count * heads_all, -1)
    mixture = jnp.dot(rounded, all_keys[:, :LAT], preferred_element_type=jnp.float32)
    mixture = mixture.reshape(query_count, heads_all, LAT) / row_total
    live_rows = (query_index < blk_length)[:, None, None]
    return jnp.where(live_rows, mixture, 0.0).astype(jnp.bfloat16).reshape(query_count, heads_all * LAT)


def finished_cache(pre_keys, new_keys, pre_length, blk_length):
    position = jnp.arange(CACHE, dtype=jnp.int32)
    pre_rows = jnp.take(pre_keys, jnp.minimum(position, PREFIX - 1), axis=0)
    offset = position - pre_length
    new_rows = jnp.take(new_keys, jnp.clip(offset, 0, BLOCK - 1), axis=0)
    in_prefix = (position < pre_length)[:, None]
    in_new = ((offset >= 0) & (offset < blk_length))[:, None]
    blank_rows = jnp.zeros_like(pre_rows)
    return jnp.where(in_prefix, pre_rows, jnp.where(in_new, new_rows, blank_rows))


def reference(queries, block_latent, prefix_cache, queue_list, prefix_len, block_len, decode_dest):
    def one_group(group_index):
        request = queue_list[group_index]
        pre_keys = lax.dynamic_index_in_dim(prefix_cache, request, 0, keepdims=False)
        new_keys = lax.dynamic_index_in_dim(block_latent, group_index, 0, keepdims=False)
        pre_length = prefix_len[request]
        blk_length = block_len[group_index]
        all_keys = jnp.concatenate([pre_keys, new_keys], axis=0)
        group_queries = lax.dynamic_index_in_dim(queries, group_index, 0, keepdims=False)
        latent = group_attention(group_queries, all_keys, pre_length, blk_length)
        return latent, finished_cache(pre_keys, new_keys, pre_length, blk_length)

    latent_out, caches = lax.map(one_group, jnp.arange(GROUPS, dtype=jnp.int32))
    hit_table = (decode_dest[:, None] == jnp.arange(GROUPS, dtype=jnp.int32)[None, :]).astype(jnp.int32)
    rank_table = jnp.cumsum(hit_table, axis=0) - hit_table
    rank = jnp.sum(rank_table * hit_table, axis=1)
    place_index = decode_dest * MOST + rank
    selector = (jnp.arange(GROUPS * MOST, dtype=jnp.int32)[:, None] == place_index[None, :]).astype(jnp.float32)
    routed = jnp.einsum('ag,gcw->acw', selector, caches.astype(jnp.float32))
    decode_pages = routed.reshape(GROUPS, MOST, PAGES, PG, KEY_W).astype(jnp.bfloat16)
    return latent_out, decode_pages
```

```python
import functools
import math

import jax
import jax.numpy as jnp
from jax import lax
from jax.experimental import pallas as pl
from jax.experimental.pallas import tpu as pltpu
from jax.sharding import PartitionSpec as P

LAT = 512
ROPE = 64
KEY_W = LAT + ROPE
PAIR_W = 2 * KEY_W
WIDE = LAT + 2 * ROPE
QK = 192
PG = 64
MOST = 2
DIRECT = 8
EXPONENT = QK**-0.5 * math.log2(math.e)
VMEM_LIMIT = 48 * 2**20


def lane_index():
    return lax.axis_index("tp") * lax.axis_size("sp") + lax.axis_index("sp")


def fill_keys(keys, pre, new, sources):
    me = lax.axis_index("pool")
    rows = pre[0].shape[-2]
    if len(pre) == 1:
        for s in range(sources):
            keys[s * rows : (s + 1) * rows, :] = pre[0][s]
    else:
        for s in range(sources):
            source = lax.rem(me - s + sources, sources)
            keys[pl.ds(pl.multiple_of(source * rows, rows), rows), :] = pre[s][0]
    first = sources * rows
    rows = new[0].shape[-2]
    for s, piece in enumerate(new):
        source = lane_index() ^ s
        keys[pl.ds(pl.multiple_of(first + source * rows, rows), rows), :] = piece[0]
    return first


def pick_prefix(queue, cache, *outs):
    me = lax.axis_index("pool")
    count = cache.shape[0]
    if len(outs) == 1:
        for s in range(count):
            outs[0][s] = cache[queue[s]]
    else:
        for s, out in enumerate(outs):
            out[0] = cache[queue[lax.rem(me + s, count)]]


def build_rows(queue, pre_len, blk_len, *refs, sources, pre_count):
    pre, new, out, keys = refs[:pre_count], refs[pre_count:-2], refs[-2], refs[-1]
    first = fill_keys(keys, pre, new, sources)
    me = lax.axis_index("pool")
    pre_length = pre_len[queue[me]]
    blk_length = blk_len[me]
    rows_lane = PG // (lax.axis_size("tp") * lax.axis_size("sp"))
    shape = (out.shape[1], keys.shape[0])
    row = lax.broadcasted_iota(jnp.int32, shape, 0)
    column = lax.broadcasted_iota(jnp.int32, shape, 1)
    position = row // rows_lane * PG + lane_index() * rows_lane + row % rows_lane
    offset = position - pre_length
    chosen = jnp.where(
        offset < 0, position, jnp.where(offset < blk_length, offset + first, -1)
    )
    picker = jnp.where(column == chosen, 1.0, 0.0).astype(jnp.bfloat16)
    out[0] = jnp.dot(picker, keys[...], preferred_element_type=jnp.float32).astype(out.dtype)


def land_rows(dest, *refs, sources):
    pieces, out = refs[:-1], refs[-1]
    me = lax.axis_index("pool")
    out[...] = jnp.zeros_like(out)
    rank = jnp.int32(0)
    for g in range(sources):
        hit = dest[g] == me

        @pl.when(hit)
        def _(g=g, rank=rank):
            if len(pieces) == 1:
                out[0, rank] = pieces[0][g]
            else:
                shift = lax.rem(me - g + sources, sources)
                for s, piece in enumerate(pieces):

                    @pl.when(shift == s)
                    def _(piece=piece):
                        out[0, rank] = piece[0]

        rank = rank + hit.astype(jnp.int32)


def attend(queue, pre_len, blk_len, queries, *refs, sources, pre_count, pairs):
    pre, new = refs[:pre_count], refs[pre_count:-5]
    out, keys, even_keys, odd_keys, bias = refs[-5:]
    me = lax.axis_index("pool")
    count = queries.shape[1]
    blk_length = blk_len[me]
    first_query = lax.axis_index("sp") * count

    @pl.when(pl.program_id(0) == 0)
    def _():
        first = fill_keys(keys, pre, new, sources)
        held = keys[...]
        blank = jnp.zeros((held.shape[0], ROPE), held.dtype)
        even_keys[...] = jnp.concatenate([held, blank], axis=1).T
        odd_keys[...] = jnp.concatenate([blank, held], axis=1).T
        row = lax.broadcasted_iota(jnp.int32, bias.shape, 0) + first_query
        column = lax.broadcasted_iota(jnp.int32, bias.shape, 1)
        index = column - first
        visible = ((index < 0) & (column < pre_len[queue[me]])) | (
            (index >= 0) & (index <= row) & (index < blk_length)
        )
        bias[...] = jnp.where(visible, 0.0, -jnp.inf)

    values = keys[:, :LAT]
    row = lax.broadcasted_iota(jnp.int32, (count, 1), 0) + first_query
    live = jnp.concatenate([row] * pairs, axis=0) < blk_length
    masked = jnp.concatenate([bias[...]] * pairs, axis=0)
    for odd, key_columns in ((0, even_keys), (1, odd_keys)):
        begin = odd * LAT
        rows = jnp.concatenate(
            [queries[0, :, p * PAIR_W + begin : p * PAIR_W + begin + WIDE] for p in range(pairs)],
            axis=0,
        )
        scores = jnp.dot(rows, key_columns[...], preferred_element_type=jnp.float32) + masked
        top = jnp.max(scores, axis=1, keepdims=True)
        weights = jnp.exp2((scores - top) * EXPONENT)
        total = jnp.sum(weights, axis=1, keepdims=True)
        mixture = jnp.dot(weights.astype(values.dtype), values, preferred_element_type=jnp.float32)
        mixture = (mixture * jnp.where(live, 1.0 / total, 0.0)).astype(out.dtype)
        for p in range(pairs):
            at = (2 * p + odd) * LAT
            out[0, :, at : at + LAT] = mixture[p * count : (p + 1) * count]


def body(queries, block_latent, prefix_cache, queue_list, prefix_len, block_len, decode_dest):
    sources = lax.axis_size("pool")
    lanes = lax.axis_size("tp") * lax.axis_size("sp")
    count, width = queries.shape[1:]
    heads = width // KEY_W
    rows_in = prefix_cache.shape[1]
    key_count = rows_in * sources + block_latent.shape[1] * lanes
    page_count = key_count // PG
    rows_lane = PG // lanes
    direct = sources <= DIRECT
    smem = pl.BlockSpec(memory_space=pltpu.SMEM)
    vmem = pl.BlockSpec(memory_space=pltpu.VMEM)
    params = pltpu.CompilerParams(vmem_limit_bytes=VMEM_LIMIT)
    dtype = queries.dtype

    def shifted(piece, s):
        pairs = [(i, (i + s) % sources) for i in range(sources)]
        return lax.ppermute(piece, "pool", pairs)

    piece = (1 if direct else sources, rows_in, KEY_W)
    pieces = sources if direct else 1
    chosen = pl.pallas_call(
        pick_prefix,
        in_specs=[smem, vmem],
        out_specs=[vmem] * pieces,
        out_shape=[jax.ShapeDtypeStruct(piece, dtype)] * pieces,
        compiler_params=params,
        name="pick_prefix",
    )(queue_list, prefix_cache)
    if direct:
        pre = [chosen[0]] + [shifted(chosen[s], s) for s in range(1, sources)]
    else:
        pre = [lax.all_to_all(chosen[0], "pool", split_axis=0, concat_axis=0, tiled=True)]
    new = [block_latent] + [
        lax.ppermute(block_latent, ("tp", "sp"), [(i, i ^ s) for i in range(lanes)])
        for s in range(1, lanes)
    ]
    scalars = (queue_list, prefix_len, block_len)
    lane_rows = pl.pallas_call(
        functools.partial(build_rows, sources=sources, pre_count=len(pre)),
        in_specs=[smem] * 3 + [vmem] * (len(pre) + len(new)),
        out_specs=vmem,
        out_shape=jax.ShapeDtypeStruct((1, page_count * rows_lane, KEY_W), dtype),
        scratch_shapes=[pltpu.VMEM((key_count, KEY_W), dtype)],
        compiler_params=params,
        name="build_rows",
    )(*scalars, *pre, *new)
    if direct:
        landed = [lane_rows] + [shifted(lane_rows, s) for s in range(1, sources)]
    else:
        landed = [lax.all_gather(lane_rows, "pool", axis=0, tiled=True)]
    pairs = heads // 2
    while pairs > 1 and pairs * count * key_count > 1024 * 384:
        pairs //= 2
    latent_out = pl.pallas_call(
        functools.partial(attend, sources=sources, pre_count=len(pre), pairs=pairs),
        grid=(heads // 2 // pairs,),
        in_specs=[smem] * 3
        + [pl.BlockSpec((1, count, pairs * PAIR_W), lambda i: (0, 0, i))]
        + [vmem] * (len(pre) + len(new)),
        out_specs=pl.BlockSpec((1, count, pairs * 2 * LAT), lambda i: (0, 0, i)),
        out_shape=jax.ShapeDtypeStruct((1, count, heads * LAT), dtype),
        scratch_shapes=[
            pltpu.VMEM((key_count, KEY_W), dtype),
            pltpu.VMEM((WIDE, key_count), dtype),
            pltpu.VMEM((WIDE, key_count), dtype),
            pltpu.VMEM((count, key_count), jnp.float32),
        ],
        compiler_params=params,
        cost_estimate=pl.CostEstimate(
            flops=2 * count * heads * key_count * (KEY_W + LAT),
            bytes_accessed=2 * count * heads * (KEY_W + LAT),
            transcendentals=count * heads * key_count,
        ),
        name="attend",
    )(*scalars, queries, *pre, *new)
    decode_pages = pl.pallas_call(
        functools.partial(land_rows, sources=sources),
        in_specs=[smem] + [vmem] * len(landed),
        out_specs=vmem,
        out_shape=jax.ShapeDtypeStruct((1, MOST, page_count * rows_lane, KEY_W), dtype),
        compiler_params=params,
        name="land_rows",
    )(decode_dest, *landed)
    return latent_out, decode_pages.reshape(1, MOST, page_count, rows_lane, KEY_W)


def solution(mesh):
    in_specs = (
        P(("parts", "pool"), "sp", "tp"),
        P(("parts", "pool"), ("tp", "sp"), None),
        P("parts", "pool", None),
        P("parts"),
        P("parts"),
        P("parts"),
        P("parts"),
    )
    out_specs = (
        P(("parts", "pool"), "sp", "tp"),
        P(("parts", "pool"), None, None, ("tp", "sp"), None),
    )
    return jax.shard_map(body, mesh=mesh, in_specs=in_specs, out_specs=out_specs, check_vma=False)
```

```python
import functools
import math

import jax
import jax.numpy as jnp
from jax import lax
from jax.experimental import pallas as pl
from jax.experimental.pallas import tpu as pltpu
from jax.sharding import PartitionSpec as P

LAT = 512
ROPE = 64
KEY_W = LAT + ROPE
PAIR_W = 2 * KEY_W
WIDE = LAT + 2 * ROPE
QK = 192
PG = 64
MOST = 2
DIRECT = 8
EXPONENT = QK**-0.5 * math.log2(math.e)
VMEM_LIMIT = 48 * 2**20


def lane_index():
    return lax.axis_index("tp") * lax.axis_size("sp") + lax.axis_index("sp")


def fill_keys(keys, pre, new, sources):
    me = lax.axis_index("pool")
    rows = pre[0].shape[-2]
    if len(pre) == 1:
        for s in range(sources):
            keys[s * rows : (s + 1) * rows, :] = pre[0][s]
    else:
        for s in range(sources):
            source = lax.rem(me - s + sources, sources)
            keys[pl.ds(pl.multiple_of(source * rows, rows), rows), :] = pre[s][0]
    first = sources * rows
    rows = new[0].shape[-2]
    for s, piece in enumerate(new):
        source = lane_index() ^ s
        keys[pl.ds(pl.multiple_of(first + source * rows, rows), rows), :] = piece[0]
    return first


def pick_prefix(queue, pre_len, blk_len, dest, cache, block, facts, own, *refs):
    outs, (lists, held, signals) = refs[:-3], refs[-3:]
    me = lax.axis_index("pool")
    count = cache.shape[0]
    copies = [
        pltpu.make_async_copy(source, lists.at[i], signals.at[i])
        for i, source in enumerate((queue, pre_len, blk_len, dest))
    ]
    copies.append(pltpu.make_async_copy(cache, held, signals.at[4]))
    copies.append(pltpu.make_async_copy(block, own, signals.at[5]))
    for copy in copies:
        copy.start()
    for copy in copies:
        copy.wait()
    if len(outs) == 1:
        for s in range(count):
            outs[0][s] = held[lists[0, s]]
    else:
        for s, out in enumerate(outs):
            out[0] = held[lists[0, lax.rem(me + s, count)]]
    facts[0] = lists[1, lists[0, me]]
    facts[1] = lists[2, me]
    for slot in range(MOST):
        facts[2 + slot] = jnp.int32(-1)
    rank = jnp.int32(0)
    for g in range(count):
        hit = lists[3, g] == me

        @pl.when(hit)
        def _(g=g, rank=rank):
            facts[2 + rank] = lax.rem(me - g + count, count)

        rank = rank + hit.astype(jnp.int32)


def build_rows(facts, *refs, sources, pre_count):
    pre, new, out, keys = refs[:pre_count], refs[pre_count:-2], refs[-2], refs[-1]
    first = fill_keys(keys, pre, new, sources)
    pre_length = facts[0]
    blk_length = facts[1]
    rows_lane = PG // (lax.axis_size("tp") * lax.axis_size("sp"))
    shape = (out.shape[1], keys.shape[0])
    row = lax.broadcasted_iota(jnp.int32, shape, 0)
    column = lax.broadcasted_iota(jnp.int32, shape, 1)
    position = row // rows_lane * PG + lane_index() * rows_lane + row % rows_lane
    offset = position - pre_length
    chosen = jnp.where(
        offset < 0, position, jnp.where(offset < blk_length, offset + first, -1)
    )
    picker = jnp.where(column == chosen, 1.0, 0.0).astype(jnp.bfloat16)
    out[0] = jnp.dot(picker, keys[...], preferred_element_type=jnp.float32).astype(out.dtype)


def land_rows(facts, *refs, sources):
    pieces, (out, blank, signals) = refs[:-3], refs[-3:]
    me = lax.axis_index("pool")
    blank[...] = jnp.zeros_like(blank)

    def landing(slot, source):
        return pltpu.make_async_copy(source, out.at[0, slot], signals.at[slot])

    for slot in range(MOST):
        shift = facts[2 + slot]

        @pl.when(shift < 0)
        def _(slot=slot):
            landing(slot, blank).start()

        if len(pieces) == 1:

            @pl.when(shift >= 0)
            def _(slot=slot, shift=shift):
                landing(slot, pieces[0].at[lax.rem(me - shift + sources, sources)]).start()
        else:
            for s, piece in enumerate(pieces):

                @pl.when(shift == s)
                def _(slot=slot, piece=piece):
                    landing(slot, piece.at[0]).start()

    for slot in range(MOST):
        landing(slot, blank).wait()


def attend(facts, queries, *refs, sources, pre_count, pairs):
    pre, new = refs[:pre_count], refs[pre_count:-7]
    out, held, keys, even_keys, odd_keys, bias, signals = refs[-7:]
    count = queries.shape[1]
    heads = queries.shape[2] // KEY_W
    blk_length = facts[1]
    first_query = lax.axis_index("sp") * count
    first = fill_keys(keys, pre, new, sources)
    blank = jnp.zeros((keys.shape[0], ROPE), keys.dtype)
    even_keys[:, :KEY_W] = keys[...]
    even_keys[:, KEY_W:] = blank
    odd_keys[...] = jnp.concatenate([blank, keys[...]], axis=1)
    row = lax.broadcasted_iota(jnp.int32, bias.shape, 0) + first_query
    column = lax.broadcasted_iota(jnp.int32, bias.shape, 1)
    index = column - first
    visible = ((index < 0) & (column < facts[0])) | (
        (index >= 0) & (index <= row) & (index < blk_length)
    )
    bias[...] = jnp.where(visible, 0.0, -jnp.inf)
    values = keys[:, :LAT]
    row = lax.broadcasted_iota(jnp.int32, (count, 1), 0) + first_query
    live = jnp.concatenate([row] * pairs, axis=0) < blk_length
    masked = jnp.concatenate([bias[...]] * pairs, axis=0)

    def leaving(head):
        columns = pl.ds(head * LAT, LAT)
        return pltpu.make_async_copy(held.at[:, columns], out.at[0, :, columns], signals.at[head])

    units = [(p, odd) for p in range(0, heads // 2, pairs) for odd in (0, 1)]
    for number, (pair, odd) in enumerate(units):
        starts = [(pair + p) * PAIR_W + odd * LAT for p in range(pairs)]
        rows = jnp.concatenate([queries[0, :, at : at + WIDE] for at in starts], axis=0)
        scores = lax.dot_general(
            rows,
            (odd_keys if odd else even_keys)[...],
            (((1,), (1,)), ((), ())),
            preferred_element_type=jnp.float32,
        )
        scores = scores + masked
        top = jnp.max(scores, axis=1, keepdims=True)
        weights = jnp.exp2((scores - top) * EXPONENT)
        scale = jnp.where(live, 1.0 / jnp.sum(weights, axis=1, keepdims=True), 0.0)
        weights = weights.astype(values.dtype)
        step = pairs if number + 1 < len(units) else max(pairs // 4, 1)
        for p in range(0, pairs, step):
            part = slice(p * count, (p + step) * count)
            mixture = jnp.dot(weights[part], values, preferred_element_type=jnp.float32)
            mixture = (mixture * scale[part]).astype(held.dtype)
            for i in range(step):
                head = 2 * (pair + p + i) + odd
                held[:, head * LAT : (head + 1) * LAT] = mixture[i * count : (i + 1) * count]
                leaving(head).start()
    for head in range(heads):
        leaving(head).wait()


def body(queries, block_latent, prefix_cache, queue_list, prefix_len, block_len, decode_dest):
    sources = lax.axis_size("pool")
    lanes = lax.axis_size("tp") * lax.axis_size("sp")
    count, width = queries.shape[1:]
    heads = width // KEY_W
    rows_in = prefix_cache.shape[1]
    key_count = rows_in * sources + block_latent.shape[1] * lanes
    page_count = key_count // PG
    rows_lane = PG // lanes
    direct = sources <= DIRECT
    smem = pl.BlockSpec(memory_space=pltpu.SMEM)
    vmem = pl.BlockSpec(memory_space=pltpu.VMEM)
    hbm = pl.BlockSpec(memory_space=pltpu.HBM)
    params = pltpu.CompilerParams(vmem_limit_bytes=VMEM_LIMIT)
    dtype = queries.dtype

    def shifted(piece, s):
        pairs = [(i, (i + s) % sources) for i in range(sources)]
        return lax.ppermute(piece, "pool", pairs)

    piece = (1 if direct else sources, rows_in, KEY_W)
    pieces = sources if direct else 1
    facts, own, *chosen = pl.pallas_call(
        pick_prefix,
        in_specs=[hbm] * 6,
        out_specs=[smem] + [vmem] * (1 + pieces),
        out_shape=[
            jax.ShapeDtypeStruct((2 + MOST,), jnp.int32),
            jax.ShapeDtypeStruct(block_latent.shape, dtype),
        ]
        + [jax.ShapeDtypeStruct(piece, dtype)] * pieces,
        scratch_shapes=[
            pltpu.SMEM((4, sources), jnp.int32),
            pltpu.VMEM(prefix_cache.shape, dtype),
            pltpu.SemaphoreType.DMA((6,)),
        ],
        compiler_params=pltpu.CompilerParams(vmem_limit_bytes=60 * 2**20),
        name="pick_prefix",
    )(queue_list, prefix_len, block_len, decode_dest, prefix_cache, block_latent)
    if direct:
        pre = [chosen[0]] + [shifted(chosen[s], s) for s in range(1, sources)]
    else:
        pre = [lax.all_to_all(chosen[0], "pool", split_axis=0, concat_axis=0, tiled=True)]
    new = [own] + [
        lax.ppermute(own, ("tp", "sp"), [(i, i ^ s) for i in range(lanes)])
        for s in range(1, lanes)
    ]
    lane_rows = pl.pallas_call(
        functools.partial(build_rows, sources=sources, pre_count=len(pre)),
        in_specs=[smem] + [vmem] * (len(pre) + len(new)),
        out_specs=vmem,
        out_shape=jax.ShapeDtypeStruct((1, page_count * rows_lane, KEY_W), dtype),
        scratch_shapes=[pltpu.VMEM((key_count, KEY_W), dtype)],
        compiler_params=params,
        cost_estimate=pl.CostEstimate(flops=4 * 10**9, bytes_accessed=10**7, transcendentals=0),
        name="build_rows",
    )(facts, *pre, *new)
    if direct:
        landed = [lane_rows] + [shifted(lane_rows, s) for s in range(1, sources)]
    else:
        landed = [lax.all_gather(lane_rows, "pool", axis=0, tiled=True)]
    pairs = heads // 2
    while pairs > 1 and pairs * count * key_count > 1024 * 384:
        pairs //= 2
    latent_out = pl.pallas_call(
        functools.partial(attend, sources=sources, pre_count=len(pre), pairs=pairs),
        in_specs=[smem] + [vmem] * (1 + len(pre) + len(new)),
        out_specs=hbm,
        out_shape=jax.ShapeDtypeStruct((1, count, heads * LAT), dtype),
        scratch_shapes=[
            pltpu.VMEM((count, heads * LAT), dtype),
            pltpu.VMEM((key_count, KEY_W), dtype),
            pltpu.VMEM((key_count, WIDE), dtype),
            pltpu.VMEM((key_count, WIDE), dtype),
            pltpu.VMEM((count, key_count), jnp.float32),
            pltpu.SemaphoreType.DMA((heads,)),
        ],
        compiler_params=params,
        cost_estimate=pl.CostEstimate(
            flops=2 * count * heads * key_count * (KEY_W + LAT),
            bytes_accessed=2 * count * heads * (KEY_W + LAT),
            transcendentals=count * heads * key_count,
        ),
        name="attend",
    )(facts, queries, *pre, *new)
    decode_pages = pl.pallas_call(
        functools.partial(land_rows, sources=sources),
        in_specs=[smem] + [vmem] * len(landed),
        out_specs=hbm,
        out_shape=jax.ShapeDtypeStruct((1, MOST, page_count * rows_lane, KEY_W), dtype),
        scratch_shapes=[
            pltpu.VMEM((page_count * rows_lane, KEY_W), dtype),
            pltpu.SemaphoreType.DMA((MOST,)),
        ],
        compiler_params=params,
        name="land_rows",
    )(facts, *landed)
    return latent_out, decode_pages.reshape(1, MOST, page_count, rows_lane, KEY_W)


def solution(mesh):
    in_specs = (
        P(("parts", "pool"), "sp", "tp"),
        P(("parts", "pool"), ("tp", "sp"), None),
        P("parts", "pool", None),
        P("parts"),
        P("parts"),
        P("parts"),
        P("parts"),
    )
    out_specs = (
        P(("parts", "pool"), "sp", "tp"),
        P(("parts", "pool"), None, None, ("tp", "sp"), None),
    )
    return jax.shard_map(body, mesh=mesh, in_specs=in_specs, out_specs=out_specs, check_vma=False)
```

```python
import functools
import math

import jax
import jax.numpy as jnp
from jax import lax
from jax.experimental import pallas as pl
from jax.experimental.pallas import tpu as pltpu
from jax.sharding import PartitionSpec as P

LAT = 512
ROPE = 64
KEY_W = LAT + ROPE
PAIR_W = 2 * KEY_W
WIDE = LAT + 2 * ROPE
QK = 192
PG = 64
MOST = 2
DIRECT = 8
EXPONENT = QK**-0.5 * math.log2(math.e)
VMEM_LIMIT = 48 * 2**20
VMEM_FIRST = 60 * 2**20


def lane_index():
    return lax.axis_index("tp") * lax.axis_size("sp") + lax.axis_index("sp")


def lane_count():
    return lax.axis_size("tp") * lax.axis_size("sp")


def shift_of(source, sources):
    return lax.rem(lax.axis_index("pool") - source + sources, sources)


def slot_groups(dest, target, sources):
    found = [jnp.int32(-1)] * MOST
    rank = jnp.int32(0)
    for g in range(sources):
        hit = dest[g] == target
        for slot in range(MOST):
            found[slot] = jnp.where(hit & (rank == slot), g, found[slot])
        rank = rank + hit.astype(jnp.int32)
    return found


def lane_positions(slots):
    rows_lane = PG // lane_count()
    return slots // rows_lane * PG + lane_index() * rows_lane + slots % rows_lane


def slots_before(length, pages):
    rows_lane = PG // lane_count()
    total = jnp.int32(0)
    for m in range(pages):
        total = total + jnp.clip(length - m * PG - lane_index() * rows_lane, 0, rows_lane)
    return total


def new_index(columns, rows):
    return (lane_index() ^ (columns // rows)) * rows + columns % rows


def pick_prefix(queue, dest, cache, *refs):
    outs, (lists, held, signals) = refs[:-3], refs[-3:]
    me = lax.axis_index("pool")
    count, rows = cache.shape[:2]
    copies = [
        pltpu.make_async_copy(source, target, signals.at[i])
        for i, (source, target) in enumerate(
            ((queue, lists.at[0]), (dest, lists.at[1]), (cache, held))
        )
    ]
    for copy in copies:
        copy.start()
    for copy in copies:
        copy.wait()
    if len(outs) == 1:
        for s in range(count):
            outs[0][s] = held[lists[0, s]]
        return
    rows_lane = PG // lane_count()
    begin = pl.multiple_of(lax.rem(lane_index() * rows_lane, rows), rows_lane)
    for s, out in enumerate(outs, 1):
        target = lax.rem(me + s, count)
        out[0, :rows] = held[lists[0, target]]
        groups = slot_groups(lists.at[1], target, count)
        for slot, group in enumerate(groups):
            request = lists[0, jnp.maximum(group, 0)]
            at = rows + slot * rows_lane
            out[0, at : at + rows_lane] = held[request, pl.ds(begin, rows_lane)]


def build_new(queue, pre_len, blk_len, *refs, pages):
    new, out = refs[:-1], refs[-1]
    me = lax.axis_index("pool")
    pre_length = pre_len[queue[me]]
    rows = new[0].shape[1]
    shape = (out.shape[1], rows * len(new))
    slot = lax.broadcasted_iota(jnp.int32, shape, 0) + slots_before(pre_length, pages)
    offset = lane_positions(slot) - pre_length
    index = new_index(lax.broadcasted_iota(jnp.int32, shape, 1), rows)
    picker = jnp.where((index == offset) & (offset < blk_len[me]), 1.0, 0.0)
    held = jnp.concatenate([piece[0] for piece in new], axis=0)
    out[0] = jnp.dot(
        picker.astype(held.dtype), held, preferred_element_type=jnp.float32
    ).astype(out.dtype)


def land_slots(queue, pre_len, dest, cache, *refs, sources):
    pre, landed = refs[: sources - 1], refs[sources - 1 : 2 * sources - 1]
    out, held, built, signals = refs[2 * sources - 1 :]
    me = lax.axis_index("pool")
    rows = cache.shape[1]
    rows_lane = PG // lane_count()
    pages = sources * rows // PG
    new_rows = landed[0].shape[1]
    first = lane_index() * rows_lane
    begin = pl.multiple_of(lax.rem(first, rows), rows_lane)
    copies = []
    for slot, group in enumerate(slot_groups(dest, me, sources)):
        request = queue[jnp.maximum(group, 0)]
        pre_length = jnp.where(group < 0, 0, pre_len[request])
        for g in range(sources):
            for s, piece in enumerate(landed):

                @pl.when((group == g) & (shift_of(g, sources) == s))
                def _(piece=piece, slot=slot):
                    held[slot, :new_rows] = piece[0]

        @pl.when(group < 0)
        def _(slot=slot):
            held[slot, :new_rows] = jnp.zeros((new_rows, KEY_W), held.dtype)

        for m in range(pages):
            shift = shift_of((m * PG + first) // rows, sources)
            at = new_rows + m * rows_lane

            @pl.when(shift == 0)
            def _(at=at, slot=slot, request=request):
                held[slot, at : at + rows_lane] = cache[request, pl.ds(begin, rows_lane)]

            for s, piece in enumerate(pre, 1):

                @pl.when(shift == s)
                def _(at=at, slot=slot, piece=piece):
                    start = rows + slot * rows_lane
                    held[slot, at : at + rows_lane] = piece[0, start : start + rows_lane]

        shape = (built.shape[1], held.shape[1])
        row = lax.broadcasted_iota(jnp.int32, shape, 0)
        column = lax.broadcasted_iota(jnp.int32, shape, 1)
        behind = row - slots_before(pre_length, pages)
        chosen = jnp.where(
            behind < 0, row + new_rows, jnp.where(behind < new_rows, behind, -1)
        )
        picker = jnp.where(column == chosen, 1.0, 0.0).astype(held.dtype)
        built[slot] = jnp.dot(
            picker, held[slot], preferred_element_type=jnp.float32
        ).astype(built.dtype)
        copies.append(pltpu.make_async_copy(built.at[slot], out.at[0, slot], signals.at[slot]))
        copies[-1].start()
    for copy in copies:
        copy.wait()


def build_rows(queue, pre_len, blk_len, pre, *refs):
    new, out = refs[:-1], refs[-1]
    me = lax.axis_index("pool")
    pre_length = pre_len[queue[me]]
    first = pre.shape[0] * pre.shape[1]
    rows = new[0].shape[1]
    held = jnp.concatenate(
        [pre[s] for s in range(pre.shape[0])] + [piece[0] for piece in new], axis=0
    )
    shape = (out.shape[1], held.shape[0])
    position = lane_positions(lax.broadcasted_iota(jnp.int32, shape, 0))
    column = lax.broadcasted_iota(jnp.int32, shape, 1)
    offset = position - pre_length
    index = new_index(jnp.maximum(column - first, 0), rows)
    picked = ((offset < 0) & (column == position)) | (
        (offset >= 0) & (offset < blk_len[me]) & (column >= first) & (index == offset)
    )
    picker = jnp.where(picked, 1.0, 0.0).astype(held.dtype)
    out[0] = jnp.dot(picker, held, preferred_element_type=jnp.float32).astype(out.dtype)


def land_rows(dest, landed, out, blank, signals):
    me = lax.axis_index("pool")
    blank[...] = jnp.zeros_like(blank)

    def landing(slot, source):
        return pltpu.make_async_copy(source, out.at[0, slot], signals.at[slot])

    for slot, group in enumerate(slot_groups(dest, me, landed.shape[0])):

        @pl.when(group < 0)
        def _(slot=slot):
            landing(slot, blank).start()

        @pl.when(group >= 0)
        def _(slot=slot, group=group):
            landing(slot, landed.at[group]).start()

    for slot in range(MOST):
        landing(slot, blank).wait()


def attend(queue, pre_len, blk_len, queries, cache, *refs, sources, pre_count, pairs):
    pre, new = refs[:pre_count], refs[pre_count:-6]
    out, held, even_keys, odd_keys, bias, signals = refs[-6:]
    me = lax.axis_index("pool")
    count = queries.shape[1]
    heads = queries.shape[2] // KEY_W
    request = queue[me]
    pre_length = pre_len[request]
    blk_length = blk_len[me]
    first_query = lax.axis_index("sp") * count
    rows = cache.shape[1]
    new_rows = new[0].shape[1]
    first = sources * rows
    column = lax.broadcasted_iota(jnp.int32, bias.shape, 1)
    if pre_count == sources - 1:
        prefix = [cache[request]] + [piece[0, :rows] for piece in pre]
        position = lax.rem(me - column // rows + sources, sources) * rows + column % rows
    else:
        prefix = [pre[0][s] for s in range(sources)]
        position = column
    keys = jnp.concatenate(prefix + [piece[0] for piece in new], axis=0)
    blank = jnp.zeros((keys.shape[0], ROPE), keys.dtype)
    even_keys[...] = jnp.concatenate([keys, blank], axis=1)
    odd_keys[...] = jnp.concatenate([blank, keys], axis=1)
    row = lax.broadcasted_iota(jnp.int32, bias.shape, 0) + first_query
    index = new_index(jnp.maximum(column - first, 0), new_rows)
    visible = ((column < first) & (position < pre_length)) | (
        (column >= first) & (index <= row) & (index < blk_length)
    )
    bias[...] = jnp.where(visible, 0.0, -jnp.inf)
    values = even_keys[:, :LAT]
    row = lax.broadcasted_iota(jnp.int32, (count, 1), 0) + first_query
    live = jnp.concatenate([row] * pairs, axis=0) < blk_length
    masked = jnp.concatenate([bias[...]] * pairs, axis=0)

    def leaving(head):
        columns = pl.ds(head * LAT, LAT)
        return pltpu.make_async_copy(held.at[:, columns], out.at[0, :, columns], signals.at[head])

    units = [(p, odd) for p in range(0, heads // 2, pairs) for odd in (0, 1)]
    for number, (pair, odd) in enumerate(units):
        starts = [(pair + p) * PAIR_W + odd * LAT for p in range(pairs)]
        some = jnp.concatenate([queries[0, :, at : at + WIDE] for at in starts], axis=0)
        scores = lax.dot_general(
            some,
            (odd_keys if odd else even_keys)[...],
            (((1,), (1,)), ((), ())),
            preferred_element_type=jnp.float32,
        )
        scores = scores + masked
        top = jnp.max(scores, axis=1, keepdims=True)
        weights = jnp.exp2((scores - top) * EXPONENT)
        scale = jnp.where(live, 1.0 / jnp.sum(weights, axis=1, keepdims=True), 0.0)
        weights = weights.astype(values.dtype)
        step = pairs if number + 1 < len(units) else max(pairs // 4, 1)
        for p in range(0, pairs, step):
            part = slice(p * count, (p + step) * count)
            mixture = jnp.dot(weights[part], values, preferred_element_type=jnp.float32)
            mixture = (mixture * scale[part]).astype(held.dtype)
            for i in range(step):
                head = 2 * (pair + p + i) + odd
                held[:, head * LAT : (head + 1) * LAT] = mixture[i * count : (i + 1) * count]
                leaving(head).start()
    for head in range(heads):
        leaving(head).wait()


def body(queries, block_latent, prefix_cache, queue_list, prefix_len, block_len, decode_dest):
    sources = lax.axis_size("pool")
    lanes = lax.axis_size("tp") * lax.axis_size("sp")
    count, width = queries.shape[1:]
    heads = width // KEY_W
    rows_in = prefix_cache.shape[1]
    pre_total = rows_in * sources
    key_count = pre_total + block_latent.shape[1] * lanes
    rows_lane = PG // lanes
    lane_total = key_count // lanes
    direct = sources <= DIRECT and PG % rows_in == 0 and rows_in % rows_lane == 0
    smem = pl.BlockSpec(memory_space=pltpu.SMEM)
    vmem = pl.BlockSpec(memory_space=pltpu.VMEM)
    hbm = pl.BlockSpec(memory_space=pltpu.HBM)
    params = pltpu.CompilerParams(vmem_limit_bytes=VMEM_LIMIT)
    dtype = queries.dtype

    def shifted(piece, s):
        pairs = [(i, (i + s) % sources) for i in range(sources)]
        return lax.ppermute(piece, "pool", pairs)

    if direct:
        pieces, piece = sources - 1, (1, rows_in + MOST * rows_lane, KEY_W)
    else:
        pieces, piece = 1, (sources, rows_in, KEY_W)
    chosen = pl.pallas_call(
        pick_prefix,
        in_specs=[hbm] * 3,
        out_specs=[vmem] * pieces,
        out_shape=[jax.ShapeDtypeStruct(piece, dtype)] * pieces,
        scratch_shapes=[
            pltpu.SMEM((2, sources), jnp.int32),
            pltpu.VMEM(prefix_cache.shape, dtype),
            pltpu.SemaphoreType.DMA((3,)),
        ],
        compiler_params=pltpu.CompilerParams(vmem_limit_bytes=VMEM_FIRST),
        cost_estimate=pl.CostEstimate(flops=4 * 10**9, bytes_accessed=10**7, transcendentals=0),
        name="pick_prefix",
    )(queue_list, decode_dest, prefix_cache)
    if direct:
        pre = [shifted(chosen[s - 1], s) for s in range(1, sources)]
    else:
        pre = [lax.all_to_all(chosen[0], "pool", split_axis=0, concat_axis=0, tiled=True)]
    new = [block_latent] + [
        lax.ppermute(block_latent, ("tp", "sp"), [(i, i ^ s) for i in range(lanes)])
        for s in range(1, lanes)
    ]
    scalars = (queue_list, prefix_len, block_len)
    lane_new = block_latent.shape[1]
    build = functools.partial(
        pl.pallas_call,
        out_specs=vmem,
        compiler_params=params,
        cost_estimate=pl.CostEstimate(flops=4 * 10**9, bytes_accessed=10**7, transcendentals=0),
    )
    if direct:
        lane_rows = build(
            functools.partial(build_new, pages=pre_total // PG),
            in_specs=[smem] * 3 + [vmem] * len(new),
            out_shape=jax.ShapeDtypeStruct((1, lane_new, KEY_W), dtype),
            name="build_new",
        )(*scalars, *new)
        landed = [lane_rows] + [shifted(lane_rows, s) for s in range(1, sources)]
    else:
        lane_rows = build(
            build_rows,
            in_specs=[smem] * 3 + [vmem] * (1 + len(new)),
            out_shape=jax.ShapeDtypeStruct((1, lane_total, KEY_W), dtype),
            name="build_rows",
        )(*scalars, *pre, *new)
        landed = [lax.all_gather(lane_rows, "pool", axis=0, tiled=True)]
    pairs = heads // 2
    while pairs > 1 and pairs * count * key_count > 1024 * 384:
        pairs //= 2
    latent_out = pl.pallas_call(
        functools.partial(attend, sources=sources, pre_count=len(pre), pairs=pairs),
        in_specs=[smem] * 3 + [vmem] * (2 + len(pre) + len(new)),
        out_specs=hbm,
        out_shape=jax.ShapeDtypeStruct((1, count, heads * LAT), dtype),
        scratch_shapes=[
            pltpu.VMEM((count, heads * LAT), dtype),
            pltpu.VMEM((key_count, WIDE), dtype),
            pltpu.VMEM((key_count, WIDE), dtype),
            pltpu.VMEM((count, key_count), jnp.float32),
            pltpu.SemaphoreType.DMA((heads,)),
        ],
        compiler_params=params,
        cost_estimate=pl.CostEstimate(
            flops=2 * count * heads * key_count * (KEY_W + LAT),
            bytes_accessed=2 * count * heads * (KEY_W + LAT),
            transcendentals=count * heads * key_count,
        ),
        name="attend",
    )(*scalars, queries, prefix_cache, *pre, *new)
    land = functools.partial(
        pl.pallas_call,
        out_specs=hbm,
        out_shape=jax.ShapeDtypeStruct((1, MOST, lane_total, KEY_W), dtype),
        compiler_params=params,
    )
    if direct:
        decode_pages = land(
            functools.partial(land_slots, sources=sources),
            in_specs=[smem] * 3 + [vmem] * (1 + len(pre) + len(landed)),
            scratch_shapes=[
                pltpu.VMEM((MOST, lane_new + pre_total // lanes, KEY_W), dtype),
                pltpu.VMEM((MOST, lane_total, KEY_W), dtype),
                pltpu.SemaphoreType.DMA((MOST,)),
            ],
            name="land_slots",
        )(queue_list, prefix_len, decode_dest, prefix_cache, *pre, *landed)
    else:
        decode_pages = land(
            land_rows,
            in_specs=[smem, vmem],
            scratch_shapes=[
                pltpu.VMEM((lane_total, KEY_W), dtype),
                pltpu.SemaphoreType.DMA((MOST,)),
            ],
            name="land_rows",
        )(decode_dest, *landed)
    return latent_out, decode_pages.reshape(1, MOST, key_count // PG, rows_lane, KEY_W)


def solution(mesh):
    in_specs = (
        P(("parts", "pool"), "sp", "tp"),
        P(("parts", "pool"), ("tp", "sp"), None),
        P("parts", "pool", None),
        P("parts"),
        P("parts"),
        P("parts"),
        P("parts"),
    )
    out_specs = (
        P(("parts", "pool"), "sp", "tp"),
        P(("parts", "pool"), None, None, ("tp", "sp"), None),
    )
    return jax.shard_map(body, mesh=mesh, in_specs=in_specs, out_specs=out_specs, check_vma=False)
```

```python
import functools
import math

import jax
import jax.numpy as jnp
from jax import lax
from jax.experimental import pallas as pl
from jax.experimental.pallas import tpu as pltpu
from jax.sharding import PartitionSpec as P

LAT = 512
ROPE = 64
KEY_W = LAT + ROPE
PAIR_W = 2 * KEY_W
WIDE = LAT + 2 * ROPE
QK = 192
PG = 64
MOST = 2
EARLY = 1
ORDER = (0, 1, 2)
ORDER_INV = (0, 1, 2)
DIRECT = 8
EXPONENT = QK**-0.5 * math.log2(math.e)
VMEM_LIMIT = 48 * 2**20
VMEM_FIRST = 60 * 2**20


def lane_index():
    return lax.axis_index("tp") * lax.axis_size("sp") + lax.axis_index("sp")


def lane_count():
    return lax.axis_size("tp") * lax.axis_size("sp")


def target_of(shift, sources):
    return lax.rem(lax.axis_index("pool") + shift, sources)


def shift_of(source, sources):
    return lax.rem(lax.axis_index("pool") - source + sources, sources)


def own_begin(rows):
    rows_lane = PG // lane_count()
    return pl.multiple_of(lax.rem(lane_index() * rows_lane, rows), rows_lane)


def requests_of(queue, dest, target, sources):
    return [queue[jnp.maximum(g, 0)] for g in slot_groups(dest, target, sources)]


def slot_groups(dest, target, sources):
    found = [jnp.int32(-1)] * MOST
    rank = jnp.int32(0)
    for g in range(sources):
        hit = dest[g] == target
        for slot in range(MOST):
            found[slot] = jnp.where(hit & (rank == slot), g, found[slot])
        rank = rank + hit.astype(jnp.int32)
    return found


def split(index, size):
    if size & (size - 1):
        return index // size, index % size
    return index >> (size.bit_length() - 1), index & (size - 1)


def lane_positions(slots):
    rows_lane = PG // lane_count()
    page, row = split(slots, rows_lane)
    return page * PG + lane_index() * rows_lane + row


def slots_before(length, pages):
    rows_lane = PG // lane_count()
    total = jnp.int32(0)
    for m in range(pages):
        total = total + jnp.clip(length - m * PG - lane_index() * rows_lane, 0, rows_lane)
    return total


def new_index(columns, rows):
    piece, row = split(columns, rows)
    return (lane_index() ^ piece) * rows + row


def pick_prefix(queue, dest, cache, *refs):
    outs, (lists, held, signals) = refs[:-3], refs[-3:]
    count, rows = cache.shape[:2]
    copies = [
        pltpu.make_async_copy(source, target, signals.at[i])
        for i, (source, target) in enumerate(
            ((queue, lists.at[0]), (dest, lists.at[1]), (cache, held))
        )
    ]
    for copy in copies:
        copy.start()
    for copy in copies:
        copy.wait()
    if len(outs) == 1:
        for s in range(count):
            outs[0][s] = held[lists[0, s]]
        return
    rows_lane = PG // lane_count()
    for s, out in enumerate(outs, 1):
        target = target_of(s, count)
        out[0, :rows] = held[lists[0, target]]
        requests = requests_of(lists.at[0], lists.at[1], target, count)
        for slot in range(EARLY):
            at = rows + slot * rows_lane
            out[0, at : at + rows_lane] = held[requests[slot], pl.ds(own_begin(rows), rows_lane)]


def build_new(queue, pre_len, blk_len, dest, cache, *refs, sources):
    new, outs = refs[:-sources], refs[-sources:]
    count = cache.shape[1]
    pages = sources * count // PG
    rows_lane = PG // lane_count()
    me = lax.axis_index("pool")
    pre_length = pre_len[queue[me]]
    rows = new[0].shape[1]
    slot = lax.broadcasted_iota(jnp.int32, (rows, 1), 0) + slots_before(pre_length, pages)
    offset = lane_positions(slot) - pre_length
    offset = jnp.where(offset < blk_len[me], offset, -1)
    index = new_index(lax.broadcasted_iota(jnp.int32, (1, rows * len(new)), 1), rows)
    picker = jnp.where(index == offset, 1.0, 0.0)
    held = jnp.concatenate([piece[0] for piece in new], axis=0)
    made = jnp.dot(picker.astype(held.dtype), held, preferred_element_type=jnp.float32)
    for s, out in enumerate(outs):
        out[0, :rows] = made.astype(out.dtype)
        if s == 0:
            continue
        requests = requests_of(queue, dest, target_of(s, sources), sources)
        for slot in range(EARLY, MOST):
            at = rows + (slot - EARLY) * rows_lane
            out[0, at : at + rows_lane] = cache[requests[slot], pl.ds(own_begin(count), rows_lane)]


def land_slots(queue, pre_len, dest, cache, *refs, sources):
    pre, landed = refs[: sources - 1], refs[sources - 1 : 2 * sources - 1]
    out, built, signals = refs[2 * sources - 1 :]
    me = lax.axis_index("pool")
    requests, rows = cache.shape[:2]
    rows_lane = PG // lane_count()
    pages = sources * rows // PG
    slots = built.shape[1]
    new_rows = landed[0].shape[1]
    sent = landed[1].shape[1]
    early = EARLY * rows_lane
    blocks = [landed[0][0]] + [piece[0] for piece in landed[1:]]
    blocks += [cache[r] for r in range(requests)]
    if EARLY:
        blocks += [piece[0, rows:] for piece in pre]
    held = jnp.concatenate(blocks, axis=0)
    own_at = new_rows + (sources - 1) * sent
    early_at = own_at + requests * rows
    slot_row = lax.broadcasted_iota(jnp.int32, (slots, 1), 0)
    wanted = []
    for slot, group in enumerate(slot_groups(dest, me, sources)):
        request = queue[jnp.maximum(group, 0)]
        pre_length = jnp.where(group < 0, 0, pre_len[request])
        shift = shift_of(jnp.maximum(group, 0), sources)
        new_at = jnp.where(shift == 0, 0, new_rows + (shift - 1) * sent)
        behind = slot_row - slots_before(pre_length, pages)
        chosen = jnp.where((behind >= 0) & (behind < new_rows), behind + new_at, -1)
        for m in range(pages):
            place = m * PG + lane_index() * rows_lane
            shift = shift_of(place // rows, sources)
            if slot < EARLY:
                there = early_at + (shift - 1) * early + slot * rows_lane
            else:
                there = 2 * new_rows + (shift - 1) * sent + (slot - EARLY) * rows_lane
            there = jnp.where(shift == 0, own_at + request * rows + place % rows, there)
            inside = (slot_row >= m * rows_lane) & (slot_row < (m + 1) * rows_lane)
            chosen = jnp.where(inside & (behind < 0), slot_row - m * rows_lane + there, chosen)
        wanted.append(jnp.where(group < 0, -1, chosen))
    column = lax.broadcasted_iota(jnp.int32, (slots, held.shape[0]), 1)
    copies = []
    for slot, chosen in enumerate(wanted):
        picker = jnp.where(column == chosen, 1.0, 0.0).astype(held.dtype)
        made = jnp.dot(picker, held, preferred_element_type=jnp.float32)
        built[slot] = made.astype(built.dtype)
        copies.append(pltpu.make_async_copy(built.at[slot], out.at[0, slot], signals.at[slot]))
        copies[-1].start()
    for copy in copies:
        copy.wait()


def build_rows(queue, pre_len, blk_len, pre, *refs):
    new, out = refs[:-1], refs[-1]
    me = lax.axis_index("pool")
    pre_length = pre_len[queue[me]]
    first = pre.shape[0] * pre.shape[1]
    rows = new[0].shape[1]
    held = jnp.concatenate(
        [pre[s] for s in range(pre.shape[0])] + [piece[0] for piece in new], axis=0
    )
    shape = (out.shape[1], held.shape[0])
    position = lane_positions(lax.broadcasted_iota(jnp.int32, shape, 0))
    column = lax.broadcasted_iota(jnp.int32, shape, 1)
    offset = position - pre_length
    index = new_index(jnp.maximum(column - first, 0), rows)
    picked = ((offset < 0) & (column == position)) | (
        (offset >= 0) & (offset < blk_len[me]) & (column >= first) & (index == offset)
    )
    picker = jnp.where(picked, 1.0, 0.0).astype(held.dtype)
    out[0] = jnp.dot(picker, held, preferred_element_type=jnp.float32).astype(out.dtype)


def land_rows(dest, landed, out, blank, signals):
    me = lax.axis_index("pool")
    blank[...] = jnp.zeros_like(blank)

    def landing(slot, source):
        return pltpu.make_async_copy(source, out.at[0, slot], signals.at[slot])

    for slot, group in enumerate(slot_groups(dest, me, landed.shape[0])):

        @pl.when(group < 0)
        def _(slot=slot):
            landing(slot, blank).start()

        @pl.when(group >= 0)
        def _(slot=slot, group=group):
            landing(slot, landed.at[group]).start()

    for slot in range(MOST):
        landing(slot, blank).wait()


def attend(queue, pre_len, blk_len, queries, cache, *refs, sources, pre_count, pairs):
    pre, new = refs[:pre_count], refs[pre_count:-6]
    out, held, even_keys, odd_keys, bias, signals = refs[-6:]
    me = lax.axis_index("pool")
    count = queries.shape[1]
    heads = queries.shape[2] // KEY_W
    request = queue[me]
    pre_length = pre_len[request]
    blk_length = blk_len[me]
    first_query = lax.axis_index("sp") * count
    rows = cache.shape[1]
    new_rows = new[0].shape[1]
    first = sources * rows
    column = lax.broadcasted_iota(jnp.int32, (1, bias.shape[1]), 1)
    if pre_count == sources - 1:
        prefix = [cache[request]] + [pre[s][0, :rows] for s in ORDER_INV]
        piece, place = split(column, rows)
        position = lax.rem(me - jnp.minimum(piece, sources) + sources, sources) * rows + place
    else:
        prefix = [pre[0][s] for s in range(sources)]
        position = column
    keys = jnp.concatenate(prefix + [piece[0] for piece in new], axis=0)
    blank = jnp.zeros((keys.shape[0], ROPE), keys.dtype)
    even_keys[...] = jnp.concatenate([keys, blank], axis=1)
    odd_keys[...] = jnp.concatenate([blank, keys], axis=1)
    index = new_index(jnp.maximum(column - first, 0), new_rows)
    never = first_query + count
    since = jnp.where(
        column < first,
        jnp.where(position < pre_length, 0, never),
        jnp.where(index < blk_length, index, never),
    )
    row = lax.broadcasted_iota(jnp.int32, bias.shape, 0) + first_query
    bias[...] = jnp.where(row >= since, 0.0, -jnp.inf)
    values = even_keys[:, :LAT]
    row = lax.broadcasted_iota(jnp.int32, (count, 1), 0) + first_query
    live = jnp.concatenate([row] * pairs, axis=0) < blk_length
    masked = jnp.concatenate([bias[...]] * pairs, axis=0)

    def leaving(head):
        columns = pl.ds(head * LAT, LAT)
        return pltpu.make_async_copy(held.at[:, columns], out.at[0, :, columns], signals.at[head])

    units = [(p, odd) for p in range(0, heads // 2, pairs) for odd in (0, 1)]
    for number, (pair, odd) in enumerate(units):
        starts = [(pair + p) * PAIR_W + odd * LAT for p in range(pairs)]
        some = jnp.concatenate([queries[0, :, at : at + WIDE] for at in starts], axis=0)
        scores = lax.dot_general(
            some,
            (odd_keys if odd else even_keys)[...],
            (((1,), (1,)), ((), ())),
            preferred_element_type=jnp.float32,
        )
        scores = scores + masked
        top = jnp.max(scores, axis=1, keepdims=True)
        weights = jnp.exp2((scores - top) * EXPONENT)
        scale = jnp.where(live, 1.0 / jnp.sum(weights, axis=1, keepdims=True), 0.0)
        weights = weights.astype(values.dtype)
        step = pairs if number + 1 < len(units) else max(pairs // 4, 1)
        for p in range(0, pairs, step):
            part = slice(p * count, (p + step) * count)
            mixture = jnp.dot(weights[part], values, preferred_element_type=jnp.float32)
            mixture = (mixture * scale[part]).astype(held.dtype)
            for i in range(step):
                head = 2 * (pair + p + i) + odd
                held[:, head * LAT : (head + 1) * LAT] = mixture[i * count : (i + 1) * count]
                leaving(head).start()
    for head in range(heads):
        leaving(head).wait()


def body(queries, block_latent, prefix_cache, queue_list, prefix_len, block_len, decode_dest):
    sources = lax.axis_size("pool")
    lanes = lax.axis_size("tp") * lax.axis_size("sp")
    count, width = queries.shape[1:]
    heads = width // KEY_W
    rows_in = prefix_cache.shape[1]
    pre_total = rows_in * sources
    key_count = pre_total + block_latent.shape[1] * lanes
    rows_lane = PG // lanes
    lane_total = key_count // lanes
    direct = sources <= DIRECT and PG % rows_in == 0 and rows_in % rows_lane == 0
    smem = pl.BlockSpec(memory_space=pltpu.SMEM)
    vmem = pl.BlockSpec(memory_space=pltpu.VMEM)
    hbm = pl.BlockSpec(memory_space=pltpu.HBM)
    params = pltpu.CompilerParams(vmem_limit_bytes=VMEM_LIMIT)
    dtype = queries.dtype

    def shifted(piece, s):
        pairs = [(i, (i + s) % sources) for i in range(sources)]
        return lax.ppermute(piece, "pool", pairs)

    if direct:
        pieces, piece = sources - 1, (1, rows_in + EARLY * rows_lane, KEY_W)
    else:
        pieces, piece = 1, (sources, rows_in, KEY_W)
    chosen = pl.pallas_call(
        pick_prefix,
        in_specs=[hbm] * 3,
        out_specs=[vmem] * pieces,
        out_shape=[jax.ShapeDtypeStruct(piece, dtype)] * pieces,
        scratch_shapes=[
            pltpu.SMEM((2, sources), jnp.int32),
            pltpu.VMEM(prefix_cache.shape, dtype),
            pltpu.SemaphoreType.DMA((3,)),
        ],
        compiler_params=pltpu.CompilerParams(vmem_limit_bytes=VMEM_FIRST),
        cost_estimate=pl.CostEstimate(flops=4 * 10**9, bytes_accessed=10**7, transcendentals=0),
        name="pick_prefix",
    )(queue_list, decode_dest, prefix_cache)
    if direct:
        pre = [shifted(chosen[s - 1], s) for s in range(1, sources)]
    else:
        pre = [lax.all_to_all(chosen[0], "pool", split_axis=0, concat_axis=0, tiled=True)]
    new = [block_latent] + [
        lax.ppermute(block_latent, ("tp", "sp"), [(i, i ^ s) for i in range(lanes)])
        for s in range(1, lanes)
    ]
    scalars = (queue_list, prefix_len, block_len)
    lane_new = block_latent.shape[1]
    build = functools.partial(
        pl.pallas_call,
        compiler_params=params,
        cost_estimate=pl.CostEstimate(flops=4 * 10**9, bytes_accessed=10**7, transcendentals=0),
    )
    if direct:
        sent = lane_new + (MOST - EARLY) * rows_lane
        ready = build(
            functools.partial(build_new, sources=sources),
            in_specs=[smem] * 4 + [vmem] * (1 + len(new)),
            out_specs=[vmem] * sources,
            out_shape=[jax.ShapeDtypeStruct((1, lane_new, KEY_W), dtype)]
            + [jax.ShapeDtypeStruct((1, sent, KEY_W), dtype)] * (sources - 1),
            name="build_new",
        )(*scalars, decode_dest, prefix_cache, *new)
        landed = [ready[0]] + [shifted(ready[s], s) for s in range(1, sources)]
    else:
        lane_rows = build(
            build_rows,
            out_specs=vmem,
            in_specs=[smem] * 3 + [vmem] * (1 + len(new)),
            out_shape=jax.ShapeDtypeStruct((1, lane_total, KEY_W), dtype),
            name="build_rows",
        )(*scalars, *pre, *new)
        landed = [lax.all_gather(lane_rows, "pool", axis=0, tiled=True)]
    pairs = heads // 2
    while pairs > 1 and pairs * count * key_count > 1024 * 384:
        pairs //= 2
    latent_out = pl.pallas_call(
        functools.partial(attend, sources=sources, pre_count=len(pre), pairs=pairs),
        in_specs=[smem] * 3 + [vmem] * (2 + len(pre) + len(new)),
        out_specs=hbm,
        out_shape=jax.ShapeDtypeStruct((1, count, heads * LAT), dtype),
        scratch_shapes=[
            pltpu.VMEM((count, heads * LAT), dtype),
            pltpu.VMEM((key_count, WIDE), dtype),
            pltpu.VMEM((key_count, WIDE), dtype),
            pltpu.VMEM((count, key_count), jnp.float32),
            pltpu.SemaphoreType.DMA((heads,)),
        ],
        compiler_params=params,
        cost_estimate=pl.CostEstimate(
            flops=2 * count * heads * key_count * (KEY_W + LAT),
            bytes_accessed=2 * count * heads * (KEY_W + LAT),
            transcendentals=count * heads * key_count,
        ),
        name="attend",
    )(*scalars, queries, prefix_cache, *([pre[s] for s in ORDER] if direct else pre), *new)
    land = functools.partial(
        pl.pallas_call,
        out_specs=hbm,
        out_shape=jax.ShapeDtypeStruct((1, MOST, lane_total, KEY_W), dtype),
        compiler_params=params,
    )
    if direct:
        decode_pages = land(
            functools.partial(land_slots, sources=sources),
            in_specs=[smem] * 3 + [vmem] * (1 + len(pre) + len(landed)),
            scratch_shapes=[
                pltpu.VMEM((MOST, lane_total, KEY_W), dtype),
                pltpu.SemaphoreType.DMA((MOST,)),
            ],
            name="land_slots",
        )(queue_list, prefix_len, decode_dest, prefix_cache, *pre, *landed)
    else:
        decode_pages = land(
            land_rows,
            in_specs=[smem, vmem],
            scratch_shapes=[
                pltpu.VMEM((lane_total, KEY_W), dtype),
                pltpu.SemaphoreType.DMA((MOST,)),
            ],
            name="land_rows",
        )(decode_dest, *landed)
    return latent_out, decode_pages.reshape(1, MOST, key_count // PG, rows_lane, KEY_W)


def solution(mesh):
    in_specs = (
        P(("parts", "pool"), "sp", "tp"),
        P(("parts", "pool"), ("tp", "sp"), None),
        P("parts", "pool", None),
        P("parts"),
        P("parts"),
        P("parts"),
        P("parts"),
    )
    out_specs = (
        P(("parts", "pool"), "sp", "tp"),
        P(("parts", "pool"), None, None, ("tp", "sp"), None),
    )
    return jax.shard_map(body, mesh=mesh, in_specs=in_specs, out_specs=out_specs, check_vma=False)
```

```python
import functools
import math

import jax
import jax.numpy as jnp
from jax import lax
from jax.experimental import pallas as pl
from jax.experimental.pallas import tpu as pltpu
from jax.sharding import PartitionSpec as P

LAT = 512
ROPE = 64
KEY_W = LAT + ROPE
PAIR_W = 2 * KEY_W
WIDE = LAT + 2 * ROPE
QK = 192
PG = 64
MOST = 2
EARLY = 1
ORDER = (0, 1, 2)
ORDER_INV = (0, 1, 2)
DIRECT = 8
EXPONENT = QK**-0.5 * math.log2(math.e)
OVER_ALL = 1e30
VMEM_LIMIT = 48 * 2**20
VMEM_FIRST = 60 * 2**20


def lane_index():
    return lax.axis_index("tp") * lax.axis_size("sp") + lax.axis_index("sp")


def lane_count():
    return lax.axis_size("tp") * lax.axis_size("sp")


def target_of(shift, sources):
    return lax.rem(lax.axis_index("pool") + shift, sources)


def shift_of(source, sources):
    return lax.rem(lax.axis_index("pool") - source + sources, sources)


def own_begin(rows):
    rows_lane = PG // lane_count()
    return pl.multiple_of(lax.rem(lane_index() * rows_lane, rows), rows_lane)


def requests_of(queue, dest, target, sources):
    return [queue[jnp.maximum(g, 0)] for g in slot_groups(dest, target, sources)]


def slot_groups(dest, target, sources):
    found = [jnp.int32(-1)] * MOST
    rank = jnp.int32(0)
    for g in range(sources):
        hit = dest[g] == target
        for slot in range(MOST):
            found[slot] = jnp.where(hit & (rank == slot), g, found[slot])
        rank = rank + hit.astype(jnp.int32)
    return found


def split(index, size):
    if size & (size - 1):
        return index // size, index % size
    return index >> (size.bit_length() - 1), index & (size - 1)


def lane_positions(slots):
    rows_lane = PG // lane_count()
    page, row = split(slots, rows_lane)
    return page * PG + lane_index() * rows_lane + row


def slots_before(length, pages):
    rows_lane = PG // lane_count()
    total = jnp.int32(0)
    for m in range(pages):
        total = total + jnp.clip(length - m * PG - lane_index() * rows_lane, 0, rows_lane)
    return total


def new_index(columns, rows):
    piece, row = split(columns, rows)
    return (lane_index() ^ piece) * rows + row


def pick_prefix(queue, dest, cache, *refs):
    outs, (lists, held, signals) = refs[:-3], refs[-3:]
    count, rows = cache.shape[:2]
    copies = [
        pltpu.make_async_copy(source, target, signals.at[i])
        for i, (source, target) in enumerate(
            ((queue, lists.at[0]), (dest, lists.at[1]), (cache, held))
        )
    ]
    for copy in copies:
        copy.start()
    for copy in copies:
        copy.wait()
    if len(outs) == 1:
        for s in range(count):
            outs[0][s] = held[lists[0, s]]
        return
    rows_lane = PG // lane_count()
    for s, out in enumerate(outs, 1):
        target = target_of(s, count)
        out[0, :rows] = held[lists[0, target]]
        requests = requests_of(lists.at[0], lists.at[1], target, count)
        for slot in range(EARLY):
            at = rows + slot * rows_lane
            out[0, at : at + rows_lane] = held[requests[slot], pl.ds(own_begin(rows), rows_lane)]


def build_new(queue, pre_len, blk_len, dest, cache, *refs, sources):
    new, outs = refs[:-sources], refs[-sources:]
    count = cache.shape[1]
    pages = sources * count // PG
    rows_lane = PG // lane_count()
    me = lax.axis_index("pool")
    pre_length = pre_len[queue[me]]
    rows = new[0].shape[1]
    slot = lax.broadcasted_iota(jnp.int32, (rows, 1), 0)
    slot = jnp.where(slot < slots_before(pre_length, pages), slot + rows, slot)
    offset = lane_positions(slot) - pre_length
    offset = jnp.where(offset < blk_len[me], offset, -1)
    index = new_index(lax.broadcasted_iota(jnp.int32, (1, rows * len(new)), 1), rows)
    picker = jnp.where(index == offset, 1.0, 0.0)
    held = jnp.concatenate([piece[0] for piece in new], axis=0)
    made = jnp.dot(picker.astype(held.dtype), held, preferred_element_type=jnp.float32)
    for s, out in enumerate(outs):
        out[0, :rows] = made.astype(out.dtype)
        if s == 0:
            continue
        requests = requests_of(queue, dest, target_of(s, sources), sources)
        for slot in range(EARLY, MOST):
            at = rows + (slot - EARLY) * rows_lane
            out[0, at : at + rows_lane] = cache[requests[slot], pl.ds(own_begin(count), rows_lane)]


def land_slots(queue, pre_len, dest, cache, *refs, sources):
    pre, landed = refs[: sources - 1], refs[sources - 1 : 2 * sources - 1]
    out, front, built, signals = refs[2 * sources - 1 :]
    me = lax.axis_index("pool")
    rows = cache.shape[1]
    rows_lane = PG // lane_count()
    pages = sources * rows // PG
    new_rows = landed[0].shape[1]
    ahead = pages * rows_lane
    groups = slot_groups(dest, me, sources)
    requests = [queue[jnp.maximum(group, 0)] for group in groups]
    for m in range(pages):
        shift = shift_of((m * PG + lane_index() * rows_lane) // rows, sources)
        there = slice(m * rows_lane, (m + 1) * rows_lane)

        @pl.when(shift == 0)
        def _(there=there):
            for slot in range(MOST):
                front[slot, there] = cache[requests[slot], pl.ds(own_begin(rows), rows_lane)]

        for s in range(1, sources):

            @pl.when(shift == s)
            def _(there=there, s=s):
                for slot in range(MOST):
                    if slot < EARLY:
                        at = rows + slot * rows_lane
                        front[slot, there] = pre[s - 1][0, at : at + rows_lane]
                    else:
                        at = new_rows + (slot - EARLY) * rows_lane
                        front[slot, there] = landed[s][0, at : at + rows_lane]

    row = lax.broadcasted_iota(jnp.int32, (ahead, KEY_W), 0)
    copies = []
    for slot, group in enumerate(groups):
        before = slots_before(pre_len[requests[slot]], pages)
        shift = jnp.where(group < 0, -1, shift_of(jnp.maximum(group, 0), sources))

        @pl.when(shift < 0)
        def _(slot=slot):
            built[slot] = jnp.zeros(built.shape[1:], built.dtype)

        for s in range(sources):

            @pl.when(shift == s)
            def _(slot=slot, s=s, before=before):
                piece = landed[s]
                low = piece[0, :ahead].astype(jnp.float32)
                early = front[slot].astype(jnp.float32)
                built[slot, :ahead] = jnp.where(row < before, early, low).astype(built.dtype)
                built[slot, ahead:new_rows] = piece[0, ahead:new_rows]
                built[slot, new_rows:] = jnp.where(row < before, low, 0.0).astype(built.dtype)

        copies.append(pltpu.make_async_copy(built.at[slot], out.at[0, slot], signals.at[slot]))
        copies[-1].start()
    for copy in copies:
        copy.wait()


def build_rows(queue, pre_len, blk_len, pre, *refs):
    new, out = refs[:-1], refs[-1]
    me = lax.axis_index("pool")
    pre_length = pre_len[queue[me]]
    first = pre.shape[0] * pre.shape[1]
    rows = new[0].shape[1]
    held = jnp.concatenate(
        [pre[s] for s in range(pre.shape[0])] + [piece[0] for piece in new], axis=0
    )
    shape = (out.shape[1], held.shape[0])
    position = lane_positions(lax.broadcasted_iota(jnp.int32, shape, 0))
    column = lax.broadcasted_iota(jnp.int32, shape, 1)
    offset = position - pre_length
    index = new_index(jnp.maximum(column - first, 0), rows)
    picked = ((offset < 0) & (column == position)) | (
        (offset >= 0) & (offset < blk_len[me]) & (column >= first) & (index == offset)
    )
    picker = jnp.where(picked, 1.0, 0.0).astype(held.dtype)
    out[0] = jnp.dot(picker, held, preferred_element_type=jnp.float32).astype(out.dtype)


def land_rows(dest, landed, out, blank, signals):
    me = lax.axis_index("pool")
    blank[...] = jnp.zeros_like(blank)

    def landing(slot, source):
        return pltpu.make_async_copy(source, out.at[0, slot], signals.at[slot])

    for slot, group in enumerate(slot_groups(dest, me, landed.shape[0])):

        @pl.when(group < 0)
        def _(slot=slot):
            landing(slot, blank).start()

        @pl.when(group >= 0)
        def _(slot=slot, group=group):
            landing(slot, landed.at[group]).start()

    for slot in range(MOST):
        landing(slot, blank).wait()


def attend(queue, pre_len, blk_len, queries, cache, *refs, sources, pre_count, pairs):
    pre, new = refs[:pre_count], refs[pre_count:-6]
    out, held, even_keys, odd_keys, bias, signals = refs[-6:]
    me = lax.axis_index("pool")
    count = queries.shape[1]
    heads = queries.shape[2] // KEY_W
    request = queue[me]
    pre_length = pre_len[request]
    blk_length = blk_len[me]
    first_query = lax.axis_index("sp") * count
    rows = cache.shape[1]
    new_rows = new[0].shape[1]
    first = sources * rows
    column = lax.broadcasted_iota(jnp.int32, (1, bias.shape[1]), 1)

    def put(at, block):
        blank = jnp.zeros((block.shape[0], ROPE), block.dtype)
        even_keys[pl.ds(at, block.shape[0])] = jnp.concatenate([block, blank], axis=1)
        odd_keys[pl.ds(at, block.shape[0])] = jnp.concatenate([blank, block], axis=1)

    if pre_count == sources - 1:
        put(0, jnp.concatenate([cache[request]] + [pre[s][0, :rows] for s in ORDER_INV], axis=0))
        piece, place = split(column, rows)
        position = lax.rem(me - jnp.minimum(piece, sources) + sources, sources) * rows + place
    else:
        put(0, jnp.concatenate([pre[0][s] for s in range(sources)], axis=0))
        position = column
    row = lax.broadcasted_iota(jnp.int32, (new_rows, 1), 0)
    for s, piece in enumerate(new):
        begin = pl.multiple_of((lane_index() ^ s) * new_rows, new_rows)
        kept = (row + begin < blk_length).astype(jnp.float32)
        put(first + begin, (piece[0].astype(jnp.float32) * kept).astype(piece.dtype))
    index = column - first
    never = first_query + count
    since = jnp.where(
        index < 0,
        jnp.where(position < pre_length, 0, never),
        jnp.where(index < blk_length, index, never),
    )
    row = lax.broadcasted_iota(jnp.int32, bias.shape, 0) + first_query
    seen = jnp.where(row >= since, 0.0, -jnp.inf)
    bias[...] = jnp.where((row >= blk_length) & (index == blk_length), OVER_ALL, seen)
    def leaving(head):
        columns = pl.ds(head * LAT, LAT)
        return pltpu.make_async_copy(held.at[:, columns], out.at[0, :, columns], signals.at[head])

    def work(pair, odd, seen):
        values = even_keys[:seen, :LAT]
        mask = bias[:, :seen]
        starts = [(pair + p) * PAIR_W + odd * LAT for p in range(pairs)]
        scores = lax.dot_general(
            jnp.concatenate([queries[0, :, at : at + WIDE] for at in starts], axis=0),
            (odd_keys if odd else even_keys)[:seen],
            (((1,), (1,)), ((), ())),
            preferred_element_type=jnp.float32,
        )
        scores = scores + jnp.concatenate([mask] * pairs, axis=0)
        top = jnp.max(scores, axis=1, keepdims=True)
        weights = jnp.exp2((scores - top) * EXPONENT)
        scale = 1.0 / jnp.sum(weights, axis=1, keepdims=True)
        mixture = jnp.dot(weights.astype(values.dtype), values, preferred_element_type=jnp.float32)
        mixture = (mixture * scale).astype(held.dtype)
        for p in range(pairs):
            head = 2 * (pair + p) + odd
            held[:, head * LAT : (head + 1) * LAT] = mixture[p * count : (p + 1) * count]
            leaving(head).start()

    for part in range(lax.axis_size("sp")):

        @pl.when(lax.axis_index("sp") == part)
        def _(part=part):
            for pair in range(0, heads // 2, pairs):
                for odd in (0, 1):
                    work(pair, odd, first + (part + 1) * count)

    for head in range(heads):
        leaving(head).wait()


def body(queries, block_latent, prefix_cache, queue_list, prefix_len, block_len, decode_dest):
    sources = lax.axis_size("pool")
    lanes = lax.axis_size("tp") * lax.axis_size("sp")
    count, width = queries.shape[1:]
    heads = width // KEY_W
    rows_in = prefix_cache.shape[1]
    pre_total = rows_in * sources
    key_count = pre_total + block_latent.shape[1] * lanes
    rows_lane = PG // lanes
    lane_total = key_count // lanes
    direct = sources <= DIRECT and PG % rows_in == 0 and rows_in % rows_lane == 0
    direct = direct and pre_total // lanes <= block_latent.shape[1]
    smem = pl.BlockSpec(memory_space=pltpu.SMEM)
    vmem = pl.BlockSpec(memory_space=pltpu.VMEM)
    hbm = pl.BlockSpec(memory_space=pltpu.HBM)
    params = pltpu.CompilerParams(vmem_limit_bytes=VMEM_LIMIT)
    dtype = queries.dtype

    def shifted(piece, s):
        pairs = [(i, (i + s) % sources) for i in range(sources)]
        return lax.ppermute(piece, "pool", pairs)

    if direct:
        pieces, piece = sources - 1, (1, rows_in + EARLY * rows_lane, KEY_W)
    else:
        pieces, piece = 1, (sources, rows_in, KEY_W)
    chosen = pl.pallas_call(
        pick_prefix,
        in_specs=[hbm] * 3,
        out_specs=[vmem] * pieces,
        out_shape=[jax.ShapeDtypeStruct(piece, dtype)] * pieces,
        scratch_shapes=[
            pltpu.SMEM((2, sources), jnp.int32),
            pltpu.VMEM(prefix_cache.shape, dtype),
            pltpu.SemaphoreType.DMA((3,)),
        ],
        compiler_params=pltpu.CompilerParams(vmem_limit_bytes=VMEM_FIRST),
        cost_estimate=pl.CostEstimate(flops=4 * 10**9, bytes_accessed=10**7, transcendentals=0),
        name="pick_prefix",
    )(queue_list, decode_dest, prefix_cache)
    if direct:
        pre = [shifted(chosen[s - 1], s) for s in range(1, sources)]
    else:
        pre = [lax.all_to_all(chosen[0], "pool", split_axis=0, concat_axis=0, tiled=True)]
    new = [block_latent] + [
        lax.ppermute(block_latent, ("tp", "sp"), [(i, i ^ s) for i in range(lanes)])
        for s in range(1, lanes)
    ]
    scalars = (queue_list, prefix_len, block_len)
    lane_new = block_latent.shape[1]
    build = functools.partial(
        pl.pallas_call,
        compiler_params=params,
        cost_estimate=pl.CostEstimate(flops=4 * 10**9, bytes_accessed=10**7, transcendentals=0),
    )
    if direct:
        sent = lane_new + (MOST - EARLY) * rows_lane
        ready = build(
            functools.partial(build_new, sources=sources),
            in_specs=[smem] * 4 + [vmem] * (1 + len(new)),
            out_specs=[vmem] * sources,
            out_shape=[jax.ShapeDtypeStruct((1, lane_new, KEY_W), dtype)]
            + [jax.ShapeDtypeStruct((1, sent, KEY_W), dtype)] * (sources - 1),
            name="build_new",
        )(*scalars, decode_dest, prefix_cache, *new)
        landed = [ready[0]] + [shifted(ready[s], s) for s in range(1, sources)]
    else:
        lane_rows = build(
            build_rows,
            out_specs=vmem,
            in_specs=[smem] * 3 + [vmem] * (1 + len(new)),
            out_shape=jax.ShapeDtypeStruct((1, lane_total, KEY_W), dtype),
            name="build_rows",
        )(*scalars, *pre, *new)
        landed = [lax.all_gather(lane_rows, "pool", axis=0, tiled=True)]
    pairs = heads // 2
    while pairs > 1 and pairs * count * key_count > 1024 * 384:
        pairs //= 2
    latent_out = pl.pallas_call(
        functools.partial(attend, sources=sources, pre_count=len(pre), pairs=pairs),
        in_specs=[smem] * 3 + [vmem] * (2 + len(pre) + len(new)),
        out_specs=hbm,
        out_shape=jax.ShapeDtypeStruct((1, count, heads * LAT), dtype),
        scratch_shapes=[
            pltpu.VMEM((count, heads * LAT), dtype),
            pltpu.VMEM((key_count, WIDE), dtype),
            pltpu.VMEM((key_count, WIDE), dtype),
            pltpu.VMEM((count, key_count), jnp.float32),
            pltpu.SemaphoreType.DMA((heads,)),
        ],
        compiler_params=params,
        cost_estimate=pl.CostEstimate(
            flops=2 * count * heads * key_count * (KEY_W + LAT),
            bytes_accessed=2 * count * heads * (KEY_W + LAT),
            transcendentals=count * heads * key_count,
        ),
        name="attend",
    )(*scalars, queries, prefix_cache, *([pre[s] for s in ORDER] if direct else pre), *new)
    land = functools.partial(
        pl.pallas_call,
        out_specs=hbm,
        out_shape=jax.ShapeDtypeStruct((1, MOST, lane_total, KEY_W), dtype),
        compiler_params=params,
    )
    if direct:
        decode_pages = land(
            functools.partial(land_slots, sources=sources),
            in_specs=[smem] * 3 + [vmem] * (1 + len(pre) + len(landed)),
            scratch_shapes=[
                pltpu.VMEM((MOST, pre_total // lanes, KEY_W), dtype),
                pltpu.VMEM((MOST, lane_total, KEY_W), dtype),
                pltpu.SemaphoreType.DMA((MOST,)),
            ],
            name="land_slots",
        )(queue_list, prefix_len, decode_dest, prefix_cache, *pre, *landed)
    else:
        decode_pages = land(
            land_rows,
            in_specs=[smem, vmem],
            scratch_shapes=[
                pltpu.VMEM((lane_total, KEY_W), dtype),
                pltpu.SemaphoreType.DMA((MOST,)),
            ],
            name="land_rows",
        )(decode_dest, *landed)
    return latent_out, decode_pages.reshape(1, MOST, key_count // PG, rows_lane, KEY_W)


def solution(mesh):
    in_specs = (
        P(("parts", "pool"), "sp", "tp"),
        P(("parts", "pool"), ("tp", "sp"), None),
        P("parts", "pool", None),
        P("parts"),
        P("parts"),
        P("parts"),
        P("parts"),
    )
    out_specs = (
        P(("parts", "pool"), "sp", "tp"),
        P(("parts", "pool"), None, None, ("tp", "sp"), None),
    )
    return jax.shard_map(body, mesh=mesh, in_specs=in_specs, out_specs=out_specs, check_vma=False)
```

```python
import functools
import math

import jax
import jax.numpy as jnp
from jax import lax
from jax.experimental import pallas as pl
from jax.experimental.pallas import tpu as pltpu
from jax.sharding import PartitionSpec as P

LAT = 512
ROPE = 64
KEY_W = LAT + ROPE
PAIR_W = 2 * KEY_W
WIDE = LAT + 2 * ROPE
QK = 192
PG = 64
MOST = 2
EARLY = 1
DIRECT = 8
EXPONENT = QK**-0.5 * math.log2(math.e)
OVER_ALL = 1e30
VMEM_LIMIT = 48 * 2**20
VMEM_FIRST = 60 * 2**20


def lane_index():
    return lax.axis_index("tp") * lax.axis_size("sp") + lax.axis_index("sp")


def lane_count():
    return lax.axis_size("tp") * lax.axis_size("sp")


def target_of(s, sources):
    return lax.rem(lax.axis_index("pool") + s, sources)


def shift_of(source, sources):
    return lax.rem(lax.axis_index("pool") - source + sources, sources)


def own_begin(rows):
    rows_lane = PG // lane_count()
    return pl.multiple_of(lax.rem(lane_index() * rows_lane, rows), rows_lane)


def value(held, index):
    column = lax.broadcasted_iota(jnp.int32, held.shape, 1)
    return jnp.sum(jnp.where(column == index, held[...].astype(jnp.float32), 0.0)).astype(jnp.int32)


def entries(held):
    return [value(held, i) for i in range(held.shape[1])]


def slot_groups(dests, target):
    found = [jnp.int32(-1)] * MOST
    rank = jnp.int32(0)
    for g, dest in enumerate(dests):
        hit = dest == target
        for slot in range(MOST):
            found[slot] = jnp.where(hit & (rank == slot), g, found[slot])
        rank = rank + hit.astype(jnp.int32)
    return found


def split(index, size):
    if size & (size - 1):
        return index // size, index % size
    return index >> (size.bit_length() - 1), index & (size - 1)


def lane_positions(slots):
    rows_lane = PG // lane_count()
    page, row = split(slots, rows_lane)
    return page * PG + lane_index() * rows_lane + row


def slots_before(length, pages):
    rows_lane = PG // lane_count()
    total = jnp.int32(0)
    for m in range(pages):
        total = total + jnp.clip(length - m * PG - lane_index() * rows_lane, 0, rows_lane)
    return total


def new_index(columns, rows):
    piece, row = split(columns, rows)
    return (lane_index() ^ piece) * rows + row


def pick_prefix(queue, dest, cache, *refs):
    outs, (lists, held, signals) = refs[:-3], refs[-3:]
    count, rows = cache.shape[:2]
    copies = [
        pltpu.make_async_copy(source, target, signals.at[i])
        for i, (source, target) in enumerate(
            ((queue, lists.at[0]), (dest, lists.at[1]), (cache, held))
        )
    ]
    for copy in copies:
        copy.start()
    for copy in copies:
        copy.wait()
    if len(outs) == 1:
        for s in range(count):
            outs[0][s] = held[lists[0, s]]
        return
    rows_lane = PG // lane_count()
    for s, out in enumerate(outs, 1):
        target = target_of(s, count)
        out[0, :rows] = held[lists[0, target]]
        groups = slot_groups([lists[1, g] for g in range(count)], target)
        requests = [lists[0, jnp.maximum(g, 0)] for g in groups]
        for slot in range(EARLY):
            at = rows + slot * rows_lane
            out[0, at : at + rows_lane] = held[requests[slot], pl.ds(own_begin(rows), rows_lane)]


def build_new(queue, pre_len, blk_len, dest, cache, *refs, sources):
    new, outs = refs[:-sources], refs[-sources:]
    count = cache.shape[1]
    pages = sources * count // PG
    rows_lane = PG // lane_count()
    me = lax.axis_index("pool")
    pre_length = pre_len[queue[me]]
    blk_length = blk_len[me]
    rows = new[0].shape[1]
    slot = lax.broadcasted_iota(jnp.int32, (rows, 1), 0)
    slot = jnp.where(slot < slots_before(pre_length, pages), slot + rows, slot)
    offset = lane_positions(slot) - pre_length
    offset = jnp.where(offset < blk_length, offset, -1)
    index = new_index(lax.broadcasted_iota(jnp.int32, (1, rows * len(new)), 1), rows)
    picker = jnp.where(index == offset, 1.0, 0.0)
    held = jnp.concatenate([piece[0] for piece in new], axis=0)
    made = jnp.dot(picker.astype(held.dtype), held, preferred_element_type=jnp.float32)
    dests = [dest[g] for g in range(sources)]
    for s, out in enumerate(outs):
        out[0, :rows] = made.astype(out.dtype)
        if s == 0:
            continue
        groups = slot_groups(dests, target_of(s, sources))
        requests = [queue[jnp.maximum(g, 0)] for g in groups]
        for slot in range(EARLY, MOST):
            at = rows + (slot - EARLY) * rows_lane
            out[0, at : at + rows_lane] = cache[requests[slot], pl.ds(own_begin(count), rows_lane)]


def land_slots(queue, pre_len, dest, cache, *refs, sources):
    pre, landed = refs[: sources - 1], refs[sources - 1 : 2 * sources - 1]
    out, stack, ends, built, signals = refs[2 * sources - 1 :]
    me = lax.axis_index("pool")
    rows = cache.shape[1]
    rows_lane = PG // lane_count()
    pages = sources * rows // PG
    new_rows = landed[0].shape[1]
    ahead = pages * rows_lane
    groups = slot_groups(entries(dest), me)
    requests = [value(queue, jnp.maximum(group, 0)) for group in groups]
    for s in range(sources):
        stack[s] = landed[s][0, :new_rows]
        if s == 0:
            for slot, request in enumerate(requests):
                ends[s, slot] = cache[request, pl.ds(own_begin(rows), rows_lane)]
            continue
        for slot in range(MOST):
            piece, at = (pre[s - 1], rows) if slot < EARLY else (landed[s], new_rows)
            at += (slot if slot < EARLY else slot - EARLY) * rows_lane
            ends[s, slot] = piece[0, at : at + rows_lane]
    stack[sources] = jnp.zeros((new_rows, KEY_W), stack.dtype)
    row = lax.broadcasted_iota(jnp.int32, (ahead, KEY_W), 0)
    copies = []
    for slot, group in enumerate(groups):
        before = slots_before(value(pre_len, requests[slot]), pages)
        before = jnp.where(group < 0, 0, before)
        shift = jnp.where(group < 0, sources, shift_of(jnp.maximum(group, 0), sources))
        front = []
        for m in range(pages):
            source = (m * PG + lane_index() * rows_lane) // rows
            front.append(ends[shift_of(source, sources), slot])
        front = jnp.concatenate(front, axis=0).astype(jnp.float32)
        low = stack[shift, :ahead].astype(jnp.float32)
        built[slot, :ahead] = jnp.where(row < before, front, low).astype(built.dtype)
        built[slot, ahead:new_rows] = stack[shift, ahead:]
        built[slot, new_rows:] = jnp.where(row < before, low, 0.0).astype(built.dtype)
        copies.append(pltpu.make_async_copy(built.at[slot], out.at[0, slot], signals.at[slot]))
        copies[-1].start()
    for copy in copies:
        copy.wait()


def build_rows(queue, pre_len, blk_len, pre, *refs):
    new, out = refs[:-1], refs[-1]
    me = lax.axis_index("pool")
    pre_length = value(pre_len, value(queue, me))
    blk_length = value(blk_len, me)
    first = pre.shape[0] * pre.shape[1]
    rows = new[0].shape[1]
    held = jnp.concatenate(
        [pre[s] for s in range(pre.shape[0])] + [piece[0] for piece in new], axis=0
    )
    shape = (out.shape[1], held.shape[0])
    position = lane_positions(lax.broadcasted_iota(jnp.int32, shape, 0))
    column = lax.broadcasted_iota(jnp.int32, shape, 1)
    offset = position - pre_length
    index = new_index(jnp.maximum(column - first, 0), rows)
    picked = ((offset < 0) & (column == position)) | (
        (offset >= 0) & (offset < blk_length) & (column >= first) & (index == offset)
    )
    picker = jnp.where(picked, 1.0, 0.0).astype(held.dtype)
    out[0] = jnp.dot(picker, held, preferred_element_type=jnp.float32).astype(out.dtype)


def land_rows(dest, landed, out, blank, signals):
    me = lax.axis_index("pool")
    blank[...] = jnp.zeros_like(blank)

    def landing(slot, source):
        return pltpu.make_async_copy(source, out.at[0, slot], signals.at[slot])

    for slot, group in enumerate(slot_groups(entries(dest), me)):

        @pl.when(group < 0)
        def _(slot=slot):
            landing(slot, blank).start()

        @pl.when(group >= 0)
        def _(slot=slot, group=group):
            landing(slot, landed.at[group]).start()

    for slot in range(MOST):
        landing(slot, blank).wait()


def attend(queue, pre_len, blk_len, queries, cache, *refs, sources, pre_count, pairs):
    pre, new = refs[:pre_count], refs[pre_count:-6]
    out, held, even_keys, odd_keys, bias, signals = refs[-6:]
    me = lax.axis_index("pool")
    count = queries.shape[1]
    heads = queries.shape[2] // KEY_W
    request = value(queue, me)
    pre_length = value(pre_len, request)
    blk_length = value(blk_len, me)
    first_query = lax.axis_index("sp") * count
    rows = cache.shape[1]
    new_rows = new[0].shape[1]
    first = sources * rows
    column = lax.broadcasted_iota(jnp.int32, (1, bias.shape[1]), 1)

    def put(at, block):
        blank = jnp.zeros((block.shape[0], ROPE), block.dtype)
        even_keys[pl.ds(at, block.shape[0])] = jnp.concatenate([block, blank], axis=1)
        odd_keys[pl.ds(at, block.shape[0])] = jnp.concatenate([blank, block], axis=1)

    if pre_count == sources - 1:
        put(0, jnp.concatenate([cache[request]] + [piece[0, :rows] for piece in pre], axis=0))
        piece, place = split(column, rows)
        position = shift_of(jnp.minimum(piece, sources - 1), sources) * rows + place
    else:
        put(0, jnp.concatenate([pre[0][s] for s in range(sources)], axis=0))
        position = column
    row = lax.broadcasted_iota(jnp.int32, (new_rows, 1), 0)
    for s, piece in enumerate(new):
        begin = pl.multiple_of((lane_index() ^ s) * new_rows, new_rows)
        kept = (row + begin < blk_length).astype(jnp.float32)
        put(first + begin, (piece[0].astype(jnp.float32) * kept).astype(piece.dtype))
    index = column - first
    never = first_query + count
    since = jnp.where(
        index < 0,
        jnp.where(position < pre_length, 0, never),
        jnp.where(index < blk_length, index, never),
    )
    row = lax.broadcasted_iota(jnp.int32, bias.shape, 0) + first_query
    seen = jnp.where(row >= since, 0.0, -jnp.inf)
    bias[...] = jnp.where((row >= blk_length) & (index == blk_length), OVER_ALL, seen)
    def leaving(head):
        columns = pl.ds(head * LAT, LAT)
        return pltpu.make_async_copy(held.at[:, columns], out.at[0, :, columns], signals.at[head])

    def work(pair, odd, seen):
        values = even_keys[:seen, :LAT]
        mask = bias[:, :seen]
        starts = [(pair + p) * PAIR_W + odd * LAT for p in range(pairs)]
        scores = lax.dot_general(
            jnp.concatenate([queries[0, :, at : at + WIDE] for at in starts], axis=0),
            (odd_keys if odd else even_keys)[:seen],
            (((1,), (1,)), ((), ())),
            preferred_element_type=jnp.float32,
        )
        scores = scores + jnp.concatenate([mask] * pairs, axis=0)
        top = jnp.max(scores, axis=1, keepdims=True)
        weights = jnp.exp2((scores - top) * EXPONENT)
        scale = 1.0 / jnp.sum(weights, axis=1, keepdims=True)
        mixture = jnp.dot(weights.astype(values.dtype), values, preferred_element_type=jnp.float32)
        mixture = (mixture * scale).astype(held.dtype)
        for p in range(pairs):
            head = 2 * (pair + p) + odd
            held[:, head * LAT : (head + 1) * LAT] = mixture[p * count : (p + 1) * count]
            leaving(head).start()

    for part in range(lax.axis_size("sp")):

        @pl.when(lax.axis_index("sp") == part)
        def _(part=part):
            for pair in range(0, heads // 2, pairs):
                for odd in (0, 1):
                    work(pair, odd, first + (part + 1) * count)

    for head in range(heads):
        leaving(head).wait()


def body(queries, block_latent, prefix_cache, queue_list, prefix_len, block_len, decode_dest):
    sources = lax.axis_size("pool")
    lanes = lax.axis_size("tp") * lax.axis_size("sp")
    count, width = queries.shape[1:]
    heads = width // KEY_W
    rows_in = prefix_cache.shape[1]
    pre_total = rows_in * sources
    key_count = pre_total + block_latent.shape[1] * lanes
    rows_lane = PG // lanes
    lane_total = key_count // lanes
    direct = sources <= DIRECT and PG % rows_in == 0 and rows_in % rows_lane == 0
    direct = direct and pre_total // lanes <= block_latent.shape[1]
    smem = pl.BlockSpec(memory_space=pltpu.SMEM)
    vmem = pl.BlockSpec(memory_space=pltpu.VMEM)
    hbm = pl.BlockSpec(memory_space=pltpu.HBM)
    params = pltpu.CompilerParams(vmem_limit_bytes=VMEM_LIMIT)
    dtype = queries.dtype

    def moved(piece, s):
        pairs = [(i, (i + s) % sources) for i in range(sources)]
        return lax.ppermute(piece, "pool", pairs)

    if direct:
        pieces, piece = sources - 1, (1, rows_in + EARLY * rows_lane, KEY_W)
    else:
        pieces, piece = 1, (sources, rows_in, KEY_W)
    chosen = pl.pallas_call(
        pick_prefix,
        in_specs=[hbm] * 3,
        out_specs=[vmem] * pieces,
        out_shape=[jax.ShapeDtypeStruct(piece, dtype)] * pieces,
        scratch_shapes=[
            pltpu.SMEM((2, sources), jnp.int32),
            pltpu.VMEM(prefix_cache.shape, dtype),
            pltpu.SemaphoreType.DMA((3,)),
        ],
        compiler_params=pltpu.CompilerParams(vmem_limit_bytes=VMEM_FIRST),
        cost_estimate=pl.CostEstimate(flops=4 * 10**9, bytes_accessed=10**7, transcendentals=0),
        name="pick_prefix",
    )(queue_list, decode_dest, prefix_cache)
    if direct:
        pre = [moved(chosen[s - 1], s) for s in range(1, sources)]
    else:
        pre = [lax.all_to_all(chosen[0], "pool", split_axis=0, concat_axis=0, tiled=True)]
    new = [block_latent] + [
        lax.ppermute(block_latent, ("tp", "sp"), [(i, i ^ s) for i in range(lanes)])
        for s in range(1, lanes)
    ]
    queue_row, prefix_row, block_row, dest_row = (
        x.reshape(1, -1) for x in (queue_list, prefix_len, block_len, decode_dest)
    )
    scalars = (queue_row, prefix_row, block_row)
    lane_new = block_latent.shape[1]
    build = functools.partial(
        pl.pallas_call,
        compiler_params=params,
        cost_estimate=pl.CostEstimate(flops=4 * 10**9, bytes_accessed=10**7, transcendentals=0),
    )
    if direct:
        sent = lane_new + (MOST - EARLY) * rows_lane
        ready = build(
            functools.partial(build_new, sources=sources),
            in_specs=[smem] * 4 + [vmem] * (1 + len(new)),
            out_specs=[vmem] * sources,
            out_shape=[jax.ShapeDtypeStruct((1, lane_new, KEY_W), dtype)]
            + [jax.ShapeDtypeStruct((1, sent, KEY_W), dtype)] * (sources - 1),
            name="build_new",
        )(queue_list, prefix_len, block_len, decode_dest, prefix_cache, *new)
        landed = [ready[0]] + [moved(ready[s], s) for s in range(1, sources)]
    else:
        lane_rows = build(
            build_rows,
            out_specs=vmem,
            in_specs=[vmem] * (4 + len(new)),
            out_shape=jax.ShapeDtypeStruct((1, lane_total, KEY_W), dtype),
            name="build_rows",
        )(*scalars, *pre, *new)
        landed = [lax.all_gather(lane_rows, "pool", axis=0, tiled=True)]
    pairs = heads // 2
    while pairs > 1 and pairs * count * key_count > 1024 * 384:
        pairs //= 2
    latent_out = pl.pallas_call(
        functools.partial(attend, sources=sources, pre_count=len(pre), pairs=pairs),
        in_specs=[vmem] * (5 + len(pre) + len(new)),
        out_specs=hbm,
        out_shape=jax.ShapeDtypeStruct((1, count, heads * LAT), dtype),
        scratch_shapes=[
            pltpu.VMEM((count, heads * LAT), dtype),
            pltpu.VMEM((key_count, WIDE), dtype),
            pltpu.VMEM((key_count, WIDE), dtype),
            pltpu.VMEM((count, key_count), jnp.float32),
            pltpu.SemaphoreType.DMA((heads,)),
        ],
        compiler_params=params,
        cost_estimate=pl.CostEstimate(
            flops=2 * count * heads * key_count * (KEY_W + LAT),
            bytes_accessed=2 * count * heads * (KEY_W + LAT),
            transcendentals=count * heads * key_count,
        ),
        name="attend",
    )(*scalars, queries, prefix_cache, *pre, *new)
    land = functools.partial(
        pl.pallas_call,
        out_specs=hbm,
        out_shape=jax.ShapeDtypeStruct((1, MOST, lane_total, KEY_W), dtype),
        compiler_params=params,
    )
    if direct:
        decode_pages = land(
            functools.partial(land_slots, sources=sources),
            in_specs=[vmem] * (4 + len(pre) + len(landed)),
            scratch_shapes=[
                pltpu.VMEM((sources + 1, lane_new, KEY_W), dtype),
                pltpu.VMEM((sources, MOST, rows_lane, KEY_W), dtype),
                pltpu.VMEM((MOST, lane_total, KEY_W), dtype),
                pltpu.SemaphoreType.DMA((MOST,)),
            ],
            name="land_slots",
        )(queue_row, prefix_row, dest_row, prefix_cache, *pre, *landed)
    else:
        decode_pages = land(
            land_rows,
            in_specs=[vmem, vmem],
            scratch_shapes=[
                pltpu.VMEM((lane_total, KEY_W), dtype),
                pltpu.SemaphoreType.DMA((MOST,)),
            ],
            name="land_rows",
        )(dest_row, *landed)
    return latent_out, decode_pages.reshape(1, MOST, key_count // PG, rows_lane, KEY_W)


def solution(mesh):
    in_specs = (
        P(("parts", "pool"), "sp", "tp"),
        P(("parts", "pool"), ("tp", "sp"), None),
        P("parts", "pool", None),
        P("parts"),
        P("parts"),
        P("parts"),
        P("parts"),
    )
    out_specs = (
        P(("parts", "pool"), "sp", "tp"),
        P(("parts", "pool"), None, None, ("tp", "sp"), None),
    )
    return jax.shard_map(body, mesh=mesh, in_specs=in_specs, out_specs=out_specs, check_vma=False)
```

```python
import functools
import math

import jax
import jax.numpy as jnp
from jax import lax
from jax.experimental import pallas as pl
from jax.experimental.pallas import tpu as pltpu
from jax.sharding import PartitionSpec as P

LAT = 512
ROPE = 64
KEY_W = LAT + ROPE
PAIR_W = 2 * KEY_W
WIDE = LAT + 2 * ROPE
QK = 192
PG = 64
MOST = 2
EARLY = 1
DIRECT = 8
EXPONENT = QK**-0.5 * math.log2(math.e)
OVER_ALL = 1e30
VMEM_LIMIT = 48 * 2**20
VMEM_FIRST = 60 * 2**20


def lane_index():
    return lax.axis_index("tp") * lax.axis_size("sp") + lax.axis_index("sp")


def lane_count():
    return lax.axis_size("tp") * lax.axis_size("sp")


def target_of(s, sources):
    return lax.rem(lax.axis_index("pool") + s, sources)


def shift_of(source, sources):
    return lax.rem(lax.axis_index("pool") - source + sources, sources)


def own_begin(rows):
    rows_lane = PG // lane_count()
    return pl.multiple_of(lax.rem(lane_index() * rows_lane, rows), rows_lane)


def value(held, index):
    column = lax.broadcasted_iota(jnp.int32, held.shape, 1)
    return jnp.sum(jnp.where(column == index, held[...].astype(jnp.float32), 0.0)).astype(jnp.int32)


def entries(held):
    return [value(held, i) for i in range(held.shape[1])]


def slot_groups(dests, target):
    found = [jnp.int32(-1)] * MOST
    rank = jnp.int32(0)
    for g, dest in enumerate(dests):
        hit = dest == target
        for slot in range(MOST):
            found[slot] = jnp.where(hit & (rank == slot), g, found[slot])
        rank = rank + hit.astype(jnp.int32)
    return found


def split(index, size):
    if size & (size - 1):
        return index // size, index % size
    return index >> (size.bit_length() - 1), index & (size - 1)


def lane_positions(slots):
    rows_lane = PG // lane_count()
    page, row = split(slots, rows_lane)
    return page * PG + lane_index() * rows_lane + row


def slots_before(length, pages):
    rows_lane = PG // lane_count()
    total = jnp.int32(0)
    for m in range(pages):
        total = total + jnp.clip(length - m * PG - lane_index() * rows_lane, 0, rows_lane)
    return total


def new_index(columns, rows):
    piece, row = split(columns, rows)
    return (lane_index() ^ piece) * rows + row


def pick_prefix(queue, dest, cache, *refs):
    outs, (lists, held, signals) = refs[:-3], refs[-3:]
    count, rows = cache.shape[:2]
    copies = [
        pltpu.make_async_copy(source, target, signals.at[i])
        for i, (source, target) in enumerate(
            ((queue, lists.at[0]), (dest, lists.at[1]), (cache, held))
        )
    ]
    for copy in copies:
        copy.start()
    for copy in copies:
        copy.wait()
    if len(outs) == 1:
        for s in range(count):
            outs[0][s] = held[lists[0, s]]
        return
    rows_lane = PG // lane_count()
    for s, out in enumerate(outs, 1):
        target = target_of(s, count)
        out[0, :rows] = held[lists[0, target]]
        groups = slot_groups([lists[1, g] for g in range(count)], target)
        requests = [lists[0, jnp.maximum(g, 0)] for g in groups]
        for slot in range(EARLY):
            at = rows + slot * rows_lane
            out[0, at : at + rows_lane] = held[requests[slot], pl.ds(own_begin(rows), rows_lane)]


def build_new(queue, pre_len, blk_len, dest, cache, *refs, sources):
    new, outs = refs[:-sources], refs[-sources:]
    count = cache.shape[1]
    pages = sources * count // PG
    rows_lane = PG // lane_count()
    me = lax.axis_index("pool")
    pre_length = pre_len[queue[me]]
    blk_length = blk_len[me]
    rows = new[0].shape[1]
    slot = lax.broadcasted_iota(jnp.int32, (rows, 1), 0)
    slot = jnp.where(slot < slots_before(pre_length, pages), slot + rows, slot)
    offset = lane_positions(slot) - pre_length
    offset = jnp.where(offset < blk_length, offset, -1)
    index = new_index(lax.broadcasted_iota(jnp.int32, (1, rows * len(new)), 1), rows)
    picker = jnp.where(index == offset, 1.0, 0.0)
    held = jnp.concatenate([piece[0] for piece in new], axis=0)
    made = jnp.dot(picker.astype(held.dtype), held, preferred_element_type=jnp.float32)
    dests = [dest[g] for g in range(sources)]
    for s, out in enumerate(outs):
        out[0, :rows] = made.astype(out.dtype)
        if s == 0:
            continue
        groups = slot_groups(dests, target_of(s, sources))
        requests = [queue[jnp.maximum(g, 0)] for g in groups]
        for slot in range(EARLY, MOST):
            at = rows + (slot - EARLY) * rows_lane
            out[0, at : at + rows_lane] = cache[requests[slot], pl.ds(own_begin(count), rows_lane)]


def land_slots(queue, pre_len, dest, cache, *refs, sources):
    pre, landed = refs[: sources - 1], refs[sources - 1 : 2 * sources - 1]
    out, stack, ends, built, signals = refs[2 * sources - 1 :]
    me = lax.axis_index("pool")
    rows = cache.shape[1]
    rows_lane = PG // lane_count()
    pages = sources * rows // PG
    new_rows = landed[0].shape[1]
    ahead = pages * rows_lane
    groups = slot_groups(entries(dest), me)
    requests = [value(queue, jnp.maximum(group, 0)) for group in groups]
    for s in range(sources):
        stack[s] = landed[s][0, :new_rows]
        if s == 0:
            for slot, request in enumerate(requests):
                ends[s, slot] = cache[request, pl.ds(own_begin(rows), rows_lane)]
            continue
        for slot in range(MOST):
            piece, at = (pre[s - 1], rows) if slot < EARLY else (landed[s], new_rows)
            at += (slot if slot < EARLY else slot - EARLY) * rows_lane
            ends[s, slot] = piece[0, at : at + rows_lane]
    stack[sources] = jnp.zeros((new_rows, KEY_W), stack.dtype)
    row = lax.broadcasted_iota(jnp.int32, (ahead, KEY_W), 0)
    copies = []
    for slot, group in enumerate(groups):
        before = slots_before(value(pre_len, requests[slot]), pages)
        before = jnp.where(group < 0, 0, before)
        shift = jnp.where(group < 0, sources, shift_of(jnp.maximum(group, 0), sources))
        front = []
        for m in range(pages):
            source = (m * PG + lane_index() * rows_lane) // rows
            front.append(ends[shift_of(source, sources), slot])
        front = jnp.concatenate(front, axis=0).astype(jnp.float32)
        low = stack[shift, :ahead].astype(jnp.float32)
        built[slot, :ahead] = jnp.where(row < before, front, low).astype(built.dtype)
        built[slot, ahead:new_rows] = stack[shift, ahead:]
        built[slot, new_rows:] = jnp.where(row < before, low, 0.0).astype(built.dtype)
        copies.append(pltpu.make_async_copy(built.at[slot], out.at[0, slot], signals.at[slot]))
        copies[-1].start()
    for copy in copies:
        copy.wait()


def build_rows(queue, pre_len, blk_len, pre, *refs):
    new, out = refs[:-1], refs[-1]
    me = lax.axis_index("pool")
    pre_length = value(pre_len, value(queue, me))
    blk_length = value(blk_len, me)
    first = pre.shape[0] * pre.shape[1]
    rows = new[0].shape[1]
    held = jnp.concatenate(
        [pre[s] for s in range(pre.shape[0])] + [piece[0] for piece in new], axis=0
    )
    shape = (out.shape[1], held.shape[0])
    position = lane_positions(lax.broadcasted_iota(jnp.int32, shape, 0))
    column = lax.broadcasted_iota(jnp.int32, shape, 1)
    offset = position - pre_length
    index = new_index(jnp.maximum(column - first, 0), rows)
    picked = ((offset < 0) & (column == position)) | (
        (offset >= 0) & (offset < blk_length) & (column >= first) & (index == offset)
    )
    picker = jnp.where(picked, 1.0, 0.0).astype(held.dtype)
    out[0] = jnp.dot(picker, held, preferred_element_type=jnp.float32).astype(out.dtype)


def land_rows(dest, landed, out, blank, signals):
    me = lax.axis_index("pool")
    blank[...] = jnp.zeros_like(blank)

    def landing(slot, source):
        return pltpu.make_async_copy(source, out.at[0, slot], signals.at[slot])

    for slot, group in enumerate(slot_groups(entries(dest), me)):

        @pl.when(group < 0)
        def _(slot=slot):
            landing(slot, blank).start()

        @pl.when(group >= 0)
        def _(slot=slot, group=group):
            landing(slot, landed.at[group]).start()

    for slot in range(MOST):
        landing(slot, blank).wait()


def attend(queue, pre_len, blk_len, queries, cache, *refs, sources, pre_count, pairs):
    pre, new = refs[:pre_count], refs[pre_count:-6]
    out, held, even_keys, odd_keys, bias, signals = refs[-6:]
    me = lax.axis_index("pool")
    count = queries.shape[1]
    heads = queries.shape[2] // KEY_W
    request = value(queue, me)
    pre_length = value(pre_len, request)
    blk_length = value(blk_len, me)
    first_query = lax.axis_index("sp") * count
    rows = cache.shape[1]
    new_rows = new[0].shape[1]
    first = sources * rows
    column = lax.broadcasted_iota(jnp.int32, (1, bias.shape[1]), 1)

    def put(at, block):
        blank = jnp.zeros((block.shape[0], ROPE), block.dtype)
        even_keys[pl.ds(at, block.shape[0])] = jnp.concatenate([block, blank], axis=1)
        odd_keys[pl.ds(at, block.shape[0])] = jnp.concatenate([blank, block], axis=1)

    if pre_count == sources - 1:
        put(0, jnp.concatenate([cache[request]] + [piece[0, :rows] for piece in pre], axis=0))
        piece, place = split(column, rows)
        position = shift_of(jnp.minimum(piece, sources - 1), sources) * rows + place
    else:
        put(0, jnp.concatenate([pre[0][s] for s in range(sources)], axis=0))
        position = column
    row = lax.broadcasted_iota(jnp.int32, (new_rows, 1), 0)
    for s, piece in enumerate(new):
        begin = pl.multiple_of((lane_index() ^ s) * new_rows, new_rows)
        kept = (row + begin < blk_length).astype(jnp.float32)
        put(first + begin, (piece[0].astype(jnp.float32) * kept).astype(piece.dtype))
    index = column - first
    never = first_query + count
    since = jnp.where(
        index < 0,
        jnp.where(position < pre_length, 0, never),
        jnp.where(index < blk_length, index, never),
    )
    row = lax.broadcasted_iota(jnp.int32, bias.shape, 0) + first_query
    seen = jnp.where(row >= since, 0.0, -jnp.inf)
    bias[...] = jnp.where((row >= blk_length) & (index == blk_length), OVER_ALL, seen)
    def leaving(head):
        columns = pl.ds(head * LAT, LAT)
        return pltpu.make_async_copy(held.at[:, columns], out.at[0, :, columns], signals.at[head])

    def work(pair, odd, seen, values, mask):
        starts = [(pair + p) * PAIR_W + odd * LAT for p in range(pairs)]
        scores = lax.dot_general(
            jnp.concatenate([queries[0, :, at : at + WIDE] for at in starts], axis=0),
            (odd_keys if odd else even_keys)[:seen],
            (((1,), (1,)), ((), ())),
            preferred_element_type=jnp.float32,
        )
        scores = scores + jnp.concatenate([mask] * pairs, axis=0)
        top = jnp.max(scores, axis=1, keepdims=True)
        weights = jnp.exp2((scores - top) * EXPONENT)
        scale = 1.0 / jnp.sum(weights, axis=1, keepdims=True)
        mixture = jnp.dot(weights.astype(values.dtype), values, preferred_element_type=jnp.float32)
        mixture = (mixture * scale).astype(held.dtype)
        for p in range(pairs):
            head = 2 * (pair + p) + odd
            held[:, head * LAT : (head + 1) * LAT] = mixture[p * count : (p + 1) * count]
            leaving(head).start()

    for part in range(lax.axis_size("sp")):

        @pl.when(lax.axis_index("sp") == part)
        def _(part=part):
            seen = first + (part + 1) * count
            values, mask = even_keys[:seen, :LAT], bias[:, :seen]
            for pair in range(0, heads // 2, pairs):
                for odd in (0, 1):
                    work(pair, odd, seen, values, mask)

    for head in range(heads):
        leaving(head).wait()


def body(queries, block_latent, prefix_cache, queue_list, prefix_len, block_len, decode_dest):
    sources = lax.axis_size("pool")
    lanes = lax.axis_size("tp") * lax.axis_size("sp")
    count, width = queries.shape[1:]
    heads = width // KEY_W
    rows_in = prefix_cache.shape[1]
    pre_total = rows_in * sources
    key_count = pre_total + block_latent.shape[1] * lanes
    rows_lane = PG // lanes
    lane_total = key_count // lanes
    direct = sources <= DIRECT and PG % rows_in == 0 and rows_in % rows_lane == 0
    direct = direct and pre_total // lanes <= block_latent.shape[1]
    smem = pl.BlockSpec(memory_space=pltpu.SMEM)
    vmem = pl.BlockSpec(memory_space=pltpu.VMEM)
    hbm = pl.BlockSpec(memory_space=pltpu.HBM)
    params = pltpu.CompilerParams(vmem_limit_bytes=VMEM_LIMIT)
    dtype = queries.dtype

    def moved(piece, s):
        pairs = [(i, (i + s) % sources) for i in range(sources)]
        return lax.ppermute(piece, "pool", pairs)

    if direct:
        pieces, piece = sources - 1, (1, rows_in + EARLY * rows_lane, KEY_W)
    else:
        pieces, piece = 1, (sources, rows_in, KEY_W)
    chosen = pl.pallas_call(
        pick_prefix,
        in_specs=[hbm] * 3,
        out_specs=[vmem] * pieces,
        out_shape=[jax.ShapeDtypeStruct(piece, dtype)] * pieces,
        scratch_shapes=[
            pltpu.SMEM((2, sources), jnp.int32),
            pltpu.VMEM(prefix_cache.shape, dtype),
            pltpu.SemaphoreType.DMA((3,)),
        ],
        compiler_params=pltpu.CompilerParams(vmem_limit_bytes=VMEM_FIRST),
        cost_estimate=pl.CostEstimate(flops=4 * 10**9, bytes_accessed=10**7, transcendentals=0),
        name="pick_prefix",
    )(queue_list, decode_dest, prefix_cache)
    if direct:
        pre = [moved(chosen[s - 1], s) for s in range(1, sources)]
    else:
        pre = [lax.all_to_all(chosen[0], "pool", split_axis=0, concat_axis=0, tiled=True)]
    new = [block_latent] + [
        lax.ppermute(block_latent, ("tp", "sp"), [(i, i ^ s) for i in range(lanes)])
        for s in range(1, lanes)
    ]
    queue_row, prefix_row, block_row, dest_row = (
        x.reshape(1, -1) for x in (queue_list, prefix_len, block_len, decode_dest)
    )
    scalars = (queue_row, prefix_row, block_row)
    lane_new = block_latent.shape[1]
    build = functools.partial(
        pl.pallas_call,
        compiler_params=params,
        cost_estimate=pl.CostEstimate(flops=4 * 10**9, bytes_accessed=10**7, transcendentals=0),
    )
    if direct:
        sent = lane_new + (MOST - EARLY) * rows_lane
        ready = build(
            functools.partial(build_new, sources=sources),
            in_specs=[smem] * 4 + [vmem] * (1 + len(new)),
            out_specs=[vmem] * sources,
            out_shape=[jax.ShapeDtypeStruct((1, lane_new, KEY_W), dtype)]
            + [jax.ShapeDtypeStruct((1, sent, KEY_W), dtype)] * (sources - 1),
            name="build_new",
        )(queue_list, prefix_len, block_len, decode_dest, prefix_cache, *new)
        landed = [ready[0]] + [moved(ready[s], s) for s in range(1, sources)]
    else:
        lane_rows = build(
            build_rows,
            out_specs=vmem,
            in_specs=[vmem] * (4 + len(new)),
            out_shape=jax.ShapeDtypeStruct((1, lane_total, KEY_W), dtype),
            name="build_rows",
        )(*scalars, *pre, *new)
        landed = [lax.all_gather(lane_rows, "pool", axis=0, tiled=True)]
    pairs = heads // 2
    while pairs > 1 and pairs * count * key_count > 1024 * 384:
        pairs //= 2
    latent_out = pl.pallas_call(
        functools.partial(attend, sources=sources, pre_count=len(pre), pairs=pairs),
        in_specs=[vmem] * (5 + len(pre) + len(new)),
        out_specs=hbm,
        out_shape=jax.ShapeDtypeStruct((1, count, heads * LAT), dtype),
        scratch_shapes=[
            pltpu.VMEM((count, heads * LAT), dtype),
            pltpu.VMEM((key_count, WIDE), dtype),
            pltpu.VMEM((key_count, WIDE), dtype),
            pltpu.VMEM((count, key_count), jnp.float32),
            pltpu.SemaphoreType.DMA((heads,)),
        ],
        compiler_params=params,
        cost_estimate=pl.CostEstimate(
            flops=2 * count * heads * key_count * (KEY_W + LAT),
            bytes_accessed=2 * count * heads * (KEY_W + LAT),
            transcendentals=count * heads * key_count,
        ),
        name="attend",
    )(*scalars, queries, prefix_cache, *pre, *new)
    land = functools.partial(
        pl.pallas_call,
        out_specs=hbm,
        out_shape=jax.ShapeDtypeStruct((1, MOST, lane_total, KEY_W), dtype),
        compiler_params=params,
    )
    if direct:
        decode_pages = land(
            functools.partial(land_slots, sources=sources),
            in_specs=[vmem] * (4 + len(pre) + len(landed)),
            scratch_shapes=[
                pltpu.VMEM((sources + 1, lane_new, KEY_W), dtype),
                pltpu.VMEM((sources, MOST, rows_lane, KEY_W), dtype),
                pltpu.VMEM((MOST, lane_total, KEY_W), dtype),
                pltpu.SemaphoreType.DMA((MOST,)),
            ],
            name="land_slots",
        )(queue_row, prefix_row, dest_row, prefix_cache, *pre, *landed)
    else:
        decode_pages = land(
            land_rows,
            in_specs=[vmem, vmem],
            scratch_shapes=[
                pltpu.VMEM((lane_total, KEY_W), dtype),
                pltpu.SemaphoreType.DMA((MOST,)),
            ],
            name="land_rows",
        )(dest_row, *landed)
    return latent_out, decode_pages.reshape(1, MOST, key_count // PG, rows_lane, KEY_W)


def solution(mesh):
    in_specs = (
        P(("parts", "pool"), "sp", "tp"),
        P(("parts", "pool"), ("tp", "sp"), None),
        P("parts", "pool", None),
        P("parts"),
        P("parts"),
        P("parts"),
        P("parts"),
    )
    out_specs = (
        P(("parts", "pool"), "sp", "tp"),
        P(("parts", "pool"), None, None, ("tp", "sp"), None),
    )
    return jax.shard_map(body, mesh=mesh, in_specs=in_specs, out_specs=out_specs, check_vma=False)
```
